32 devices in a mesh: groups: 2 (over y), ctx: 4 (over z), head: 2 (over x), tp: 2 (over core).
Axes of the slice: x: 2, y: 2, z: 4, core: 2. Of those that a mesh axis runs over, the one named last changes fastest.
Arguments:
- queries: bfloat16 [32, 2048, 128], P(('head', 'tp'), ('groups', 'ctx')), parts along dimension 1, may hold values from -80 to 80
- stretch_keys: bfloat16 [8, 2048, 128], P(('head', 'tp'), ('groups', 'ctx')), parts along dimension 1, may hold values from -120 to 120
- stretch_values: bfloat16 [8, 2048, 128], P(('head', 'tp'), ('groups', 'ctx')), parts along dimension 1, may hold values from -6 to 6
- cache_keys: bfloat16 [8, 32768, 128], P(('head', 'tp'), ('groups', 'ctx')), parts along dimension 1, may hold values from -6 to 6
- cache_values: bfloat16 [8, 32768, 128], P(('head', 'tp'), ('groups', 'ctx')), parts along dimension 1, may hold values from -6 to 6
- block_picks: int32 [4, 8, 16], P('groups'), parts along dimension 0, may hold values from 0 to 31, as said below
- block_table: int32 [64], P('groups'), parts along dimension 0, may hold values from 0 to 31, as said below
Outputs:
- attended: bfloat16 [32, 2048, 128], P(('head', 'tp'), ('groups', 'ctx')), parts along dimension 1
The draws below stay inside these ranges and needn't reach their ends.
There are 2 independent parts, one for each index of `groups`. The reference program is written for one: setup_inputs(seed, part) draws one part's arguments, and reference() takes and returns one part's arrays. A program takes and returns all parts, laid end to end along the dimension named above; each array names one. Nothing has to cross between parts.
Inputs may be any that keep to these rules, and one draw needn't show every extreme that they name: `block_picks`: for each query block and KV head the 16 picks are different logical blocks; exactly 4 of them have slots on each of 4 different indices of ctx, slot s lying on index s // 8. `block_table`: A permutation of the 32 physical slots.
All inputs are finite; a program needn't handle non-finite values.
Results may differ from the reference program's by a relative error of at most 0.0032.
Values may be sent and summed in bfloat16 or wider, within the bound.
A program may use at most 64 MiB of HBM per device.

```python
import jax
import jax.numpy as jnp
from jax import lax

QH = 32
KVH = 8
HD = 128
BLOCK = 512
TOPK = 16
NBLK_DEV = 8
TOK_DEV = 256
STRETCH = 1024
QBLK = 2
CACHE_BLOCKS = 32
CAP = 4
OWNERS = 4


def query_key_pair(key):
    base = jax.random.fold_in(key, 31)
    key_q, key_k = jax.random.split(base, 2)
    queries = 2.5 * jax.random.normal(key_q, (QH, STRETCH, HD), jnp.float32)
    keys_out = jax.random.normal(key_k, (KVH, STRETCH, HD), jnp.float32)
    return (queries, keys_out)


def draw_queries(key, part):
    return query_key_pair(key)[0].astype(jnp.bfloat16)


def draw_stretch_keys(key, part):
    return query_key_pair(key)[1].astype(jnp.bfloat16)


def block_layout(key):
    base = jax.random.fold_in(key, 53)
    key_t, key_h, key_s, key_l = jax.random.split(base, 4)
    prior_token_total = CACHE_BLOCKS // NBLK_DEV
    table = jax.random.permutation(key_t, CACHE_BLOCKS).astype(jnp.int32)
    inverse = jnp.argsort(table).astype(jnp.int32)
    preferred_worker_index = jax.random.permutation(key_h, prior_token_total)
    relevance_increment = jnp.where(preferred_worker_index < max(1, prior_token_total // 8), 3000, 0).astype(jnp.int32)
    noise_perturbation = jax.random.randint(key_s, (QBLK, KVH, prior_token_total), 0, 4000, jnp.int32)
    tile_relevance = (noise_perturbation + relevance_increment[None, None, :]) * prior_token_total + jnp.arange(prior_token_total, dtype=jnp.int32)
    owners = jnp.argsort(-tile_relevance, axis=-1)[..., :OWNERS].astype(jnp.int32)
    starting = jax.random.randint(key_l, (QBLK, KVH, OWNERS, 1), 0, NBLK_DEV, jnp.int32)
    in_owner = (starting + jnp.arange(CAP, dtype=jnp.int32)) % NBLK_DEV
    physical = (owners[..., None] * NBLK_DEV + in_owner).reshape(QBLK, KVH, TOPK)
    return (table, inverse[physical].astype(jnp.int32))


def draw_block_picks(key, part):
    return block_layout(key)[1]


def draw_block_table(key, part):
    return block_layout(key)[0]


def shard_levels(own_key, shape, pieces, smallest, high):
    def one(position, parts):
        draws = jax.random.uniform(jax.random.fold_in(jax.random.fold_in(own_key, 6), position), (parts,), jnp.float32, smallest / len(pieces), high / len(pieces))
        return jnp.repeat(jnp.exp(draws), shape[position] // parts).reshape((-1,) + (1,) * (len(shape) - position - 1))

    factor_of = one(*pieces[0])
    for cut in pieces[1:]:
        factor_of = factor_of * one(*cut)
    return factor_of


def scatter_about(key, extent, width, reach, shards=(), kind=jnp.bfloat16):
    values = jax.random.normal(key, extent, jnp.float32) * width
    if len(shards) > 0:
        values = shard_levels(key, extent, shards, -0.22, 0.18) * values
    return jnp.clip(values, min=-reach, max=reach).astype(kind)


def setup_inputs(seed: int = 0, part: int = 0) -> dict:
    arg_keys = jax.random.split(jax.random.key(seed), 8)
    part_keys = jax.random.split(jax.random.fold_in(arg_keys[7], part), 8)
    return {
        "queries": draw_queries(jax.random.fold_in(jax.random.fold_in(arg_keys[7], part), 71), part),
        "stretch_keys": draw_stretch_keys(jax.random.fold_in(jax.random.fold_in(arg_keys[7], part), 71), part),
        "stretch_values": scatter_about(part_keys[2], (KVH, STRETCH, HD), 1.0, 6.0, ((0, 4), (1, 4))),
        "cache_keys": scatter_about(part_keys[3], (KVH, CACHE_BLOCKS * BLOCK, HD), 1.0, 6.0, ((0, 4), (1, 4))),
        "cache_values": scatter_about(part_keys[4], (KVH, CACHE_BLOCKS * BLOCK, HD), 1.0, 6.0, ((0, 4), (1, 4))),
        "block_picks": draw_block_picks(jax.random.fold_in(jax.random.fold_in(arg_keys[7], part), 71), part),
        "block_table": draw_block_table(jax.random.fold_in(jax.random.fold_in(arg_keys[7], part), 71), part),
    }


def reference(queries, stretch_keys, stretch_values, cache_keys, cache_values, block_picks, block_table):
    q_per_kv = QH // KVH
    tiled_keyset = cache_keys.reshape(KVH, CACHE_BLOCKS, BLOCK, HD)
    value_blocks = cache_values.reshape(KVH, CACHE_BLOCKS, BLOCK, HD)
    padded_keys = jnp.pad(stretch_keys, ((0, 0), (TOK_DEV, 0), (0, 0)))
    padded_values = jnp.pad(stretch_values, ((0, 0), (TOK_DEV, 0), (0, 0)))
    head_ids = jnp.arange(KVH, dtype=jnp.int32)[:, None]
    span_cols = TOPK * BLOCK
    columns = jnp.arange(span_cols + BLOCK + TOK_DEV, dtype=jnp.int32)
    positions = jnp.arange(BLOCK, dtype=jnp.int32)
    relative = columns[None, :] - span_cols

    def one_block(block_id):
        first_row = (block_id * BLOCK).astype(jnp.int32)
        allowed_mask = (columns[None, :] < span_cols) | ((relative <= positions[:, None] + TOK_DEV) & (relative > positions[:, None]) & (relative >= TOK_DEV - first_row))
        q_block = lax.dynamic_slice_in_dim(queries, first_row, BLOCK, 1)
        q_block = q_block.reshape(KVH, q_per_kv, BLOCK, HD).astype(jnp.float32)
        window_keys = lax.dynamic_slice_in_dim(padded_keys, first_row, BLOCK + TOK_DEV, 1)
        window_values = lax.dynamic_slice_in_dim(padded_values, first_row, BLOCK + TOK_DEV, 1)
        physical = block_table[block_picks[block_id]].astype(jnp.int32)
        selected_keyset = tiled_keyset[head_ids, physical].reshape(KVH, span_cols, HD)
        picked_values = value_blocks[head_ids, physical].reshape(KVH, span_cols, HD)
        all_keys = jnp.concatenate([selected_keyset, window_keys], axis=1).astype(jnp.float32)
        all_values = jnp.concatenate([picked_values, window_values], axis=1).astype(jnp.float32)
        tile_relevance = jnp.einsum("gqrd,gkd->gqrk", q_block, all_keys) * (HD ** -0.5)
        tile_relevance = jnp.where(allowed_mask[None, None], tile_relevance, -jnp.inf)
        row_max = jnp.max(tile_relevance, axis=-1, keepdims=True)
        weights = jnp.exp(tile_relevance - row_max)
        row_sum = jnp.sum(weights, axis=-1, keepdims=True)
        rounded = lax.optimization_barrier(weights.astype(jnp.bfloat16)).astype(jnp.float32)
        mixed = jnp.einsum("gqrk,gkd->gqrd", rounded, all_values) / row_sum
        return mixed.reshape(QH, BLOCK, HD).astype(jnp.bfloat16)

    result = lax.map(one_block, jnp.arange(QBLK, dtype=jnp.int32))
    return jnp.transpose(result, (1, 0, 2, 3)).reshape(QH, STRETCH, HD)
```

```python
import functools
import math

import jax
import jax.numpy as jnp
import numpy as np
from jax import lax
from jax.experimental import pallas as pl
from jax.experimental.pallas import tpu as pltpu
from jax.sharding import PartitionSpec as P

BLOCK = 512
TOPK = 16


def shifted(value, axis, by):
    count = lax.axis_size(axis)
    pairs = [(i, i + by) for i in range(count) if 0 <= i + by < count]
    return lax.ppermute(value, axis, pairs)


def as_sent(value):

    def short(part):
        return part.astype(jnp.bfloat16) if part.dtype == jnp.float32 else part

    return jax.tree.map(short, value)


def partner(value, axis, bit):
    mask = 2**bit
    pairs = [(source, source ^ mask) for source in range(lax.axis_size(axis))]
    return lax.ppermute(value, axis, pairs)


def lookup(lookup_table, indices):
    entries = jnp.arange(lookup_table.shape[0], dtype=jnp.int32)
    return jnp.sum(jnp.where(indices[..., None] == entries, lookup_table, 0), axis=-1)


def owner_rank(owners):
    ordinal = jnp.arange(owners.shape[-1], dtype=jnp.int32)
    before = (owners[..., :, None] == owners[..., None, :]) & (ordinal[None, :] < ordinal[:, None])
    return jnp.sum(before, axis=-1)


def pick_rows(source, indices):
    return source[indices]


def take_blocks(blocks, indices):
    return jax.vmap(pick_rows)(blocks, indices)


def attend(query_rows, all_keys, all_values, allowed_mask):
    tile_relevance = jnp.einsum(
        "rd,kd->rk", query_rows, all_keys, preferred_element_type=jnp.float32
    )
    tile_relevance = tile_relevance * query_rows.shape[-1] ** (-0.5)
    tile_relevance = jnp.where(allowed_mask, tile_relevance, -jnp.inf)
    row_max = jnp.max(tile_relevance, axis=-1, keepdims=True)
    weights = jnp.exp(tile_relevance - row_max)
    weight_sum = jnp.sum(weights, axis=-1, keepdims=True)
    mixed = jnp.einsum(
        "rk,kd->rd", weights.astype(jnp.bfloat16), all_values, preferred_element_type=jnp.float32
    )
    return (mixed / weight_sum).astype(jnp.bfloat16)


def shards(
    queries, stretch_keys, stretch_values, cache_keys, cache_values, block_picks, block_table
):
    kv_dev, tok_dev, head_dim = stretch_keys.shape
    q_per_kv = queries.shape[0] // kv_dev
    blocks_dev = cache_keys.shape[1] // BLOCK
    ctx_size = lax.axis_size("ctx")
    ctx_index = lax.axis_index("ctx")
    per_peer = max(1, TOPK // ctx_size)
    parity = ctx_index % 2
    head_ids = lax.axis_index(("head", "tp")) * kv_dev + jnp.arange(kv_dev, dtype=jnp.int32)
    selector = head_ids[:, None] == jnp.arange(block_picks.shape[1], dtype=jnp.int32)[None, :]
    my_picks = jnp.sum(jnp.where(selector[None, :, :, None], block_picks[:, None, :, :], 0), axis=2)
    physical = lookup(block_table, my_picks)
    owners = physical // blocks_dev
    in_owner = physical % blocks_dev
    peer_rank = owner_rank(owners)
    targets = np.arange(ctx_size) * tok_dev // BLOCK
    target_owner = owners[targets]
    target_rank = peer_rank[targets]
    target_local = in_owner[targets]
    slot_ids = jnp.arange(per_peer, dtype=jnp.int32)
    matched = (target_owner[:, :, None, :] == ctx_index) & (
        target_rank[:, :, None, :] == slot_ids[None, None, :, None]
    )
    chosen = jnp.sum(jnp.where(matched, target_local[:, :, None, :], 0), axis=-1)
    usable = jnp.any(matched, axis=-1)
    chosen = jnp.transpose(chosen, (1, 0, 2)).reshape(kv_dev, ctx_size * per_peer)
    usable = jnp.transpose(usable, (1, 0, 2)).reshape(kv_dev, ctx_size * per_peer)
    my_block = ctx_index * tok_dev // BLOCK
    my_owner = lax.dynamic_index_in_dim(owners, my_block, 0, keepdims=False)
    my_rank = lax.dynamic_index_in_dim(peer_rank, my_block, 0, keepdims=False)
    my_slot = my_owner * per_peer + my_rank
    prev_keys, prev_values = shifted((stretch_keys, stretch_values), "ctx", 1)
    half_rows = BLOCK // 2
    key_halves = cache_keys.reshape(kv_dev, blocks_dev * 2, half_rows, head_dim)
    value_halves = cache_values.reshape(kv_dev, blocks_dev * 2, half_rows, head_dim)
    row_side = jnp.asarray(np.repeat(np.arange(ctx_size) % 2, per_peer), jnp.int32)
    half_index = chosen * 2 + row_side[None, :]
    sent_keys = jnp.where(usable[:, :, None, None], take_blocks(key_halves, half_index), 0).astype(
        jnp.bfloat16
    )
    sent_values = jnp.where(
        usable[:, :, None, None], take_blocks(value_halves, half_index), 0
    ).astype(jnp.bfloat16)
    got_keys, got_values = (
        lax.all_to_all(sent_keys, "ctx", split_axis=1, concat_axis=1, tiled=True),
        lax.all_to_all(sent_values, "ctx", split_axis=1, concat_axis=1, tiled=True),
    )
    mine_keys = take_blocks(got_keys, my_slot)
    mine_values = take_blocks(got_values, my_slot)
    other_keys, other_values = (
        partner(as_sent(mine_keys), "ctx", 0).astype(mine_keys.dtype),
        partner(as_sent(mine_values), "ctx", 0).astype(mine_values.dtype),
    )
    first_keys = jnp.where(parity == 0, mine_keys, other_keys)
    second_keys = jnp.where(parity == 0, other_keys, mine_keys)
    first_values = jnp.where(parity == 0, mine_values, other_values)
    second_values = jnp.where(parity == 0, other_values, mine_values)
    live_keys = jnp.concatenate([first_keys, second_keys], axis=2)
    live_values = jnp.concatenate([first_values, second_values], axis=2)
    span_cols = TOPK * BLOCK
    live_keys = live_keys.reshape(kv_dev, span_cols, head_dim)
    live_values = live_values.reshape(kv_dev, span_cols, head_dim)
    all_keys = jnp.concatenate([live_keys, prev_keys, stretch_keys], axis=1)
    all_values = jnp.concatenate([live_values, prev_values, stretch_values], axis=1)
    query_rows = queries.reshape(kv_dev, q_per_kv * tok_dev, head_dim)
    step_rows = min(512, q_per_kv * tok_dev)
    columns = jnp.arange(span_cols + 2 * tok_dev, dtype=jnp.int32)

    def one_head(packed):
        q_head, k_head, v_head = packed
        q_steps = q_head.reshape(-1, step_rows, head_dim)
        starts = jnp.arange(q_steps.shape[0], dtype=jnp.int32) * step_rows

        def one_step(packed_block_step):
            q_block, first_row = packed_block_step
            position = (first_row + jnp.arange(step_rows, dtype=jnp.int32)) % tok_dev
            cache_part = columns[None, :] < span_cols
            earlier_part = (
                (columns[None, :] >= span_cols)
                & (columns[None, :] < span_cols + tok_dev)
                & (columns[None, :] - span_cols > position[:, None])
                & (ctx_index > 0)
            )
            own_part = (columns[None, :] >= span_cols + tok_dev) & (
                columns[None, :] - span_cols - tok_dev <= position[:, None]
            )
            return attend(q_block, k_head, v_head, cache_part | earlier_part | own_part)

        return lax.map(one_step, (q_steps, starts)).reshape(q_per_kv * tok_dev, head_dim)

    result = lax.map(one_head, (query_rows, all_keys, all_values))
    return result.reshape(kv_dev * q_per_kv, tok_dev, head_dim)


ROWS = 512


def fold(a, m, l, a2, m2, l2):
    top = jnp.maximum(m, m2)
    x, y = jnp.exp2(m - top), jnp.exp2(m2 - top)
    return a * x + a2 * y, top, l * x + l2 * y


def line_kernel(
    n, tok, picks_ref, table_ref, q_ref, sk_ref, sv_ref, ck_ref, cv_ref, out_ref,
    qbuf, kbuf, vbuf, skbuf, svbuf, acc, mcol, lcol, tx, txs, rxl, rxls, rxr, rxrs,
    spots, local_sem, q_right, q_left, q_recv, p_send, s_send,
    pl_recv, sl_recv, pr_recv, sr_recv,
):
    me = lax.axis_index("ctx")
    rows, head_dim = q_ref.shape
    kv_dev, blocks_dev = ck_ref.shape[:2]
    chunks = rows // ROWS
    per_head = chunks // kv_dev
    per = TOPK // n
    qblocks = picks_ref.shape[0]
    scale = head_dim ** (-0.5) * math.log2(math.e)
    mesh_id = pl.DeviceIdType.MESH
    has_left, has_right = me > 0, me < n - 1
    left, right = {"ctx": me - 1}, {"ctx": me + 1}

    def part(c):
        return pl.ds(pl.multiple_of(c * ROWS, ROWS), ROWS)

    def send_q(src, c, to, sems, own=False):
        return pltpu.make_async_remote_copy(
            src_ref=q_ref.at[part(c)] if own else qbuf.at[src, part(c)],
            dst_ref=qbuf.at[src, part(c)],
            send_sem=sems.at[src, c], recv_sem=q_recv.at[src, c],
            device_id=to, device_id_type=mesh_id,
        )

    def send_p(t, c, to, rx, rxs, sem, ssem):
        return (
            pltpu.make_async_remote_copy(
                src_ref=tx.at[t, part(c)], dst_ref=rx.at[t, part(c)],
                send_sem=p_send.at[t, c], recv_sem=sem.at[t, c],
                device_id=to, device_id_type=mesh_id,
            ),
            pltpu.make_async_remote_copy(
                src_ref=txs.at[t, c], dst_ref=rxs.at[t, c],
                send_sem=s_send.at[t, c], recv_sem=ssem.at[t, c],
                device_id=to, device_id_type=mesh_id,
            ),
        )

    to_right = (right, rxl, rxls, pl_recv, sl_recv)
    to_left = (left, rxr, rxrs, pr_recv, sr_recv)

    loads = [
        pltpu.make_async_copy(src, dst, local_sem.at[k])
        for k, (src, dst) in enumerate((
            (q_ref, qbuf.at[me]), (sk_ref, skbuf), (sv_ref, svbuf),
            (ck_ref, kbuf), (cv_ref, vbuf),
        ))
    ]
    for load in loads:
        load.start()

    barrier = pltpu.get_barrier_semaphore()

    @pl.when(has_left)
    def _():
        pl.semaphore_signal(barrier, inc=1, device_id=left, device_id_type=mesh_id)

    @pl.when(has_right)
    def _():
        pl.semaphore_signal(barrier, inc=1, device_id=right, device_id_type=mesh_id)

    pl.semaphore_wait(barrier, jnp.where(has_left, 1, 0) + jnp.where(has_right, 1, 0))

    for c in range(chunks):
        @pl.when(has_right)
        def _():
            send_q(me, c, right, q_right, True).start()

        @pl.when(has_left)
        def _():
            send_q(me, c, left, q_left, True).start()

    first_head = (lax.axis_index("head") * lax.axis_size("tp") + lax.axis_index("tp")) * kv_dev
    for j in range(qblocks):
        for g in range(kv_dev):
            found = [jnp.int32(0)] * per
            count = jnp.int32(0)
            for k in range(TOPK):
                slot = table_ref[picks_ref[j, first_head + g, k]]
                spot = slot - me * blocks_dev
                here = (spot >= 0) & (spot < blocks_dev)
                for r in range(per):
                    found[r] = jnp.where(here & (count == r), spot, found[r])
                count = count + jnp.where(here, 1, 0)
            for r in range(per):
                spots[j, g, r] = found[r]

    for load in loads:
        load.wait()

    def score(t, c, window):
        g = c // per_head
        j = t * tok // BLOCK
        picked = [spots[j, g, r] for r in range(per)]
        for h in range(ROWS // tok):
            at = pl.ds(pl.multiple_of(c * ROWS + h * tok, tok), tok)
            q = qbuf[t, at, :]
            parts = [
                lax.dot_general(
                    q, kbuf[g, spot], (((1,), (1,)), ((), ())),
                    preferred_element_type=jnp.float32,
                )
                for spot in picked
            ]
            if window:
                s = lax.dot_general(
                    q, skbuf[g], (((1,), (1,)), ((), ())),
                    preferred_element_type=jnp.float32,
                )
                row = lax.broadcasted_iota(jnp.int32, s.shape, 0)
                col = lax.broadcasted_iota(jnp.int32, s.shape, 1)
                own = jnp.where(t == me, 1, 0)
                lead = (row - col) * (2 * own - 1) + own
                parts.append(jnp.where(lead > 0, s, -jnp.inf))
            top = functools.reduce(
                jnp.maximum, [jnp.max(s, axis=1, keepdims=True) for s in parts]
            ) * scale
            total = jnp.zeros((tok, head_dim), jnp.float32)
            norm = jnp.zeros((tok, 1), jnp.float32)
            for k, s in enumerate(parts):
                w = jnp.exp2(s * scale - top)
                norm = norm + jnp.sum(w, axis=1, keepdims=True)
                v = vbuf[g, picked[k]] if k < per else svbuf[g]
                total = total + jnp.dot(
                    w.astype(jnp.bfloat16), v, preferred_element_type=jnp.float32
                )
            acc[t, at, :] = total
            mcol[t, at, :] = top
            lcol[t, at, :] = norm

    def compute(t, c):
        near = (t == me) | (t == me + 1)

        @pl.when(near)
        def _():
            score(t, c, True)

        @pl.when(jnp.logical_not(near))
        def _():
            score(t, c, False)

    eye = (
        lax.broadcasted_iota(jnp.int32, (128, 128), 0)
        == lax.broadcasted_iota(jnp.int32, (128, 128), 1)
    )

    def to_row(col):
        return jnp.sum(jnp.where(eye, col, 0.0), axis=0, keepdims=True)

    def to_col(row):
        return jnp.sum(jnp.where(eye, row, 0.0), axis=1, keepdims=True)

    cuts = ROWS // 128

    def fold_in(t, c, rx, rxs):
        for k in range(cuts):
            at = pl.ds(pl.multiple_of(c * ROWS + k * 128, 128), 128)
            a, m, l = fold(
                acc[t, at, :], mcol[t, at, :], lcol[t, at, :],
                rx[t, at, :].astype(jnp.float32),
                to_col(rxs[t, c, k:k + 1, :]), to_col(rxs[t, c, cuts + k:cuts + k + 1, :]),
            )
            acc[t, at, :] = a
            mcol[t, at, :] = m
            lcol[t, at, :] = l

    def pack(t, c):
        for k in range(cuts):
            at = pl.ds(pl.multiple_of(c * ROWS + k * 128, 128), 128)
            tx[t, at, :] = acc[t, at, :].astype(jnp.bfloat16)
            txs[t, c, k:k + 1, :] = to_row(mcol[t, at, :])
            txs[t, c, cuts + k:cuts + k + 1, :] = to_row(lcol[t, at, :])

    def hand_on(t, c, upstream, way):
        @pl.when(upstream)
        def _():
            for copy in send_p(t, c, *way):
                copy.wait_recv()
            fold_in(t, c, way[1], way[2])

        pack(t, c)
        for copy in send_p(t, c, *way):
            copy.start()

    def each(body):
        lax.fori_loop(0, chunks, lambda c, z: (body(c), z)[1], 0)

    each(lambda c: compute(me, c))

    for b in range(1, n):
        def arrive(c, b=b):
            @pl.when(me >= b)
            def _():
                send_q(me - b, c, right, q_right).wait_recv()

                @pl.when(has_right)
                def _():
                    send_q(me - b, c, right, q_right).start()

            @pl.when(me + b < n)
            def _():
                send_q(me + b, c, left, q_left).wait_recv()

                @pl.when(has_left)
                def _():
                    send_q(me + b, c, left, q_left).start()

            @pl.when(me + b < n)
            def _():
                compute(me + b, c)

            @pl.when(me >= b)
            def _():
                compute(me - b, c)

        def depart(c, b=b):
            @pl.when((b > me) & has_right)
            def _():
                hand_on(b, c, has_left, to_right)

            @pl.when((b > n - 1 - me) & has_left)
            def _():
                hand_on(n - 1 - b, c, has_right, to_left)

        each(arrive)
        each(depart)

    def finish(c):
        @pl.when(has_left)
        def _():
            for copy in send_p(me, c, *to_right):
                copy.wait_recv()
            fold_in(me, c, rxl, rxls)

        @pl.when(has_right)
        def _():
            for copy in send_p(me, c, *to_left):
                copy.wait_recv()
            fold_in(me, c, rxr, rxrs)

        out_ref[part(c), :] = (acc[me, part(c), :] / lcol[me, part(c), :]).astype(out_ref.dtype)

    each(finish)

    def drain(c):
        for s in range(n):
            @pl.when((s <= me) & has_right)
            def _():
                send_q(s, c, right, q_right).wait_send()

            @pl.when((s >= me) & has_left)
            def _():
                send_q(s, c, left, q_left).wait_send()

            @pl.when(s > me)
            def _():
                for copy in send_p(s, c, *to_right):
                    copy.wait_send()

            @pl.when(s < me)
            def _():
                for copy in send_p(s, c, *to_left):
                    copy.wait_send()

    each(drain)


def line_shards(
    queries, stretch_keys, stretch_values, cache_keys, cache_values, block_picks, block_table
):
    n = lax.axis_size("ctx")
    kv_dev, tok, head_dim = stretch_keys.shape
    rows = queries.shape[0] * tok
    chunks = rows // ROWS
    by_block = (kv_dev, cache_keys.shape[1] // BLOCK, BLOCK, head_dim)
    any_space = pl.BlockSpec(memory_space=pl.ANY)
    smem = pl.BlockSpec(memory_space=pltpu.SMEM)
    bf16, f32 = jnp.bfloat16, jnp.float32
    stats = pltpu.VMEM((n, chunks, 8, 128), f32)
    rows_bf16 = pltpu.VMEM((n, rows, head_dim), bf16)
    column = pltpu.VMEM((n, rows, 1), f32)
    sems = pltpu.SemaphoreType.DMA((n, chunks))
    result = pl.pallas_call(
        functools.partial(line_kernel, n, tok),
        out_shape=jax.ShapeDtypeStruct((rows, head_dim), bf16),
        in_specs=[smem, smem] + [any_space] * 5,
        out_specs=pl.BlockSpec(memory_space=pltpu.VMEM),
        scratch_shapes=[
            rows_bf16,
            pltpu.VMEM(by_block, bf16), pltpu.VMEM(by_block, bf16),
            pltpu.VMEM(stretch_keys.shape, bf16), pltpu.VMEM(stretch_values.shape, bf16),
            pltpu.VMEM((n, rows, head_dim), f32), column, column,
            rows_bf16, stats, rows_bf16, stats, rows_bf16, stats,
            pltpu.SMEM((block_picks.shape[0], kv_dev, TOPK // n), jnp.int32),
            pltpu.SemaphoreType.DMA((5,)),
        ] + [sems] * 9,
        compiler_params=pltpu.CompilerParams(
            collective_id=0, has_side_effects=True, vmem_limit_bytes=56 * 2**20
        ),
    )(
        block_picks, block_table, queries.reshape(rows, head_dim),
        stretch_keys, stretch_values, cache_keys.reshape(by_block), cache_values.reshape(by_block),
    )
    return result.reshape(queries.shape)


def solution(mesh):
    placed = (
        P(("head", "tp"), ("groups", "ctx"), None),
        P(("head", "tp"), ("groups", "ctx"), None),
        P(("head", "tp"), ("groups", "ctx"), None),
        P(("head", "tp"), ("groups", "ctx"), None),
        P(("head", "tp"), ("groups", "ctx"), None),
        P("groups", None, None),
        P("groups"),
    )
    few = TOPK % mesh.shape["ctx"] == 0
    return jax.shard_map(
        line_shards if few else shards,
        mesh=mesh,
        in_specs=placed,
        out_specs=P(("head", "tp"), ("groups", "ctx"), None),
        check_vma=False,
    )
```

```python
import functools
import math

import jax
import jax.numpy as jnp
import numpy as np
from jax import lax
from jax.experimental import pallas as pl
from jax.experimental.pallas import tpu as pltpu
from jax.sharding import PartitionSpec as P

BLOCK = 512
TOPK = 16


def shifted(value, axis, by):
    count = lax.axis_size(axis)
    pairs = [(i, i + by) for i in range(count) if 0 <= i + by < count]
    return lax.ppermute(value, axis, pairs)


def as_sent(value):

    def short(part):
        return part.astype(jnp.bfloat16) if part.dtype == jnp.float32 else part

    return jax.tree.map(short, value)


def partner(value, axis, bit):
    mask = 2**bit
    pairs = [(source, source ^ mask) for source in range(lax.axis_size(axis))]
    return lax.ppermute(value, axis, pairs)


def lookup(lookup_table, indices):
    entries = jnp.arange(lookup_table.shape[0], dtype=jnp.int32)
    return jnp.sum(jnp.where(indices[..., None] == entries, lookup_table, 0), axis=-1)


def owner_rank(owners):
    ordinal = jnp.arange(owners.shape[-1], dtype=jnp.int32)
    before = (owners[..., :, None] == owners[..., None, :]) & (ordinal[None, :] < ordinal[:, None])
    return jnp.sum(before, axis=-1)


def pick_rows(source, indices):
    return source[indices]


def take_blocks(blocks, indices):
    return jax.vmap(pick_rows)(blocks, indices)


def attend(query_rows, all_keys, all_values, allowed_mask):
    tile_relevance = jnp.einsum(
        "rd,kd->rk", query_rows, all_keys, preferred_element_type=jnp.float32
    )
    tile_relevance = tile_relevance * query_rows.shape[-1] ** (-0.5)
    tile_relevance = jnp.where(allowed_mask, tile_relevance, -jnp.inf)
    row_max = jnp.max(tile_relevance, axis=-1, keepdims=True)
    weights = jnp.exp(tile_relevance - row_max)
    weight_sum = jnp.sum(weights, axis=-1, keepdims=True)
    mixed = jnp.einsum(
        "rk,kd->rd", weights.astype(jnp.bfloat16), all_values, preferred_element_type=jnp.float32
    )
    return (mixed / weight_sum).astype(jnp.bfloat16)


def shards(
    queries, stretch_keys, stretch_values, cache_keys, cache_values, block_picks, block_table
):
    kv_dev, tok_dev, head_dim = stretch_keys.shape
    q_per_kv = queries.shape[0] // kv_dev
    blocks_dev = cache_keys.shape[1] // BLOCK
    ctx_size = lax.axis_size("ctx")
    ctx_index = lax.axis_index("ctx")
    per_peer = max(1, TOPK // ctx_size)
    parity = ctx_index % 2
    head_ids = lax.axis_index(("head", "tp")) * kv_dev + jnp.arange(kv_dev, dtype=jnp.int32)
    selector = head_ids[:, None] == jnp.arange(block_picks.shape[1], dtype=jnp.int32)[None, :]
    my_picks = jnp.sum(jnp.where(selector[None, :, :, None], block_picks[:, None, :, :], 0), axis=2)
    physical = lookup(block_table, my_picks)
    owners = physical // blocks_dev
    in_owner = physical % blocks_dev
    peer_rank = owner_rank(owners)
    targets = np.arange(ctx_size) * tok_dev // BLOCK
    target_owner = owners[targets]
    target_rank = peer_rank[targets]
    target_local = in_owner[targets]
    slot_ids = jnp.arange(per_peer, dtype=jnp.int32)
    matched = (target_owner[:, :, None, :] == ctx_index) & (
        target_rank[:, :, None, :] == slot_ids[None, None, :, None]
    )
    chosen = jnp.sum(jnp.where(matched, target_local[:, :, None, :], 0), axis=-1)
    usable = jnp.any(matched, axis=-1)
    chosen = jnp.transpose(chosen, (1, 0, 2)).reshape(kv_dev, ctx_size * per_peer)
    usable = jnp.transpose(usable, (1, 0, 2)).reshape(kv_dev, ctx_size * per_peer)
    my_block = ctx_index * tok_dev // BLOCK
    my_owner = lax.dynamic_index_in_dim(owners, my_block, 0, keepdims=False)
    my_rank = lax.dynamic_index_in_dim(peer_rank, my_block, 0, keepdims=False)
    my_slot = my_owner * per_peer + my_rank
    prev_keys, prev_values = shifted((stretch_keys, stretch_values), "ctx", 1)
    half_rows = BLOCK // 2
    key_halves = cache_keys.reshape(kv_dev, blocks_dev * 2, half_rows, head_dim)
    value_halves = cache_values.reshape(kv_dev, blocks_dev * 2, half_rows, head_dim)
    row_side = jnp.asarray(np.repeat(np.arange(ctx_size) % 2, per_peer), jnp.int32)
    half_index = chosen * 2 + row_side[None, :]
    sent_keys = jnp.where(usable[:, :, None, None], take_blocks(key_halves, half_index), 0).astype(
        jnp.bfloat16
    )
    sent_values = jnp.where(
        usable[:, :, None, None], take_blocks(value_halves, half_index), 0
    ).astype(jnp.bfloat16)
    got_keys, got_values = (
        lax.all_to_all(sent_keys, "ctx", split_axis=1, concat_axis=1, tiled=True),
        lax.all_to_all(sent_values, "ctx", split_axis=1, concat_axis=1, tiled=True),
    )
    mine_keys = take_blocks(got_keys, my_slot)
    mine_values = take_blocks(got_values, my_slot)
    other_keys, other_values = (
        partner(as_sent(mine_keys), "ctx", 0).astype(mine_keys.dtype),
        partner(as_sent(mine_values), "ctx", 0).astype(mine_values.dtype),
    )
    first_keys = jnp.where(parity == 0, mine_keys, other_keys)
    second_keys = jnp.where(parity == 0, other_keys, mine_keys)
    first_values = jnp.where(parity == 0, mine_values, other_values)
    second_values = jnp.where(parity == 0, other_values, mine_values)
    live_keys = jnp.concatenate([first_keys, second_keys], axis=2)
    live_values = jnp.concatenate([first_values, second_values], axis=2)
    span_cols = TOPK * BLOCK
    live_keys = live_keys.reshape(kv_dev, span_cols, head_dim)
    live_values = live_values.reshape(kv_dev, span_cols, head_dim)
    all_keys = jnp.concatenate([live_keys, prev_keys, stretch_keys], axis=1)
    all_values = jnp.concatenate([live_values, prev_values, stretch_values], axis=1)
    query_rows = queries.reshape(kv_dev, q_per_kv * tok_dev, head_dim)
    step_rows = min(512, q_per_kv * tok_dev)
    columns = jnp.arange(span_cols + 2 * tok_dev, dtype=jnp.int32)

    def one_head(packed):
        q_head, k_head, v_head = packed
        q_steps = q_head.reshape(-1, step_rows, head_dim)
        starts = jnp.arange(q_steps.shape[0], dtype=jnp.int32) * step_rows

        def one_step(packed_block_step):
            q_block, first_row = packed_block_step
            position = (first_row + jnp.arange(step_rows, dtype=jnp.int32)) % tok_dev
            cache_part = columns[None, :] < span_cols
            earlier_part = (
                (columns[None, :] >= span_cols)
                & (columns[None, :] < span_cols + tok_dev)
                & (columns[None, :] - span_cols > position[:, None])
                & (ctx_index > 0)
            )
            own_part = (columns[None, :] >= span_cols + tok_dev) & (
                columns[None, :] - span_cols - tok_dev <= position[:, None]
            )
            return attend(q_block, k_head, v_head, cache_part | earlier_part | own_part)

        return lax.map(one_step, (q_steps, starts)).reshape(q_per_kv * tok_dev, head_dim)

    result = lax.map(one_head, (query_rows, all_keys, all_values))
    return result.reshape(kv_dev * q_per_kv, tok_dev, head_dim)


ROWS = 512


def fold(a, m, l, a2, m2, l2):
    top = jnp.maximum(m, m2)
    x, y = jnp.exp2(m - top), jnp.exp2(m2 - top)
    return a * x + a2 * y, top, l * x + l2 * y


def line_kernel(
    n, tok, picks_ref, table_ref, q_ref, sk_ref, sv_ref, ck_ref, cv_ref, out_ref,
    qbuf, kbuf, vbuf, skbuf, svbuf, acc, mcol, lcol, tx, txs, rxl, rxls, rxr, rxrs,
    spots, local_sem, q_right, q_left, q_recv, p_send, s_send,
    pl_recv, sl_recv, pr_recv, sr_recv,
):
    me = lax.axis_index("ctx")
    rows, head_dim = q_ref.shape
    kv_dev, blocks_dev = ck_ref.shape[:2]
    chunks = rows // ROWS
    per_head = chunks // kv_dev
    per = TOPK // n
    qblocks = picks_ref.shape[0]
    scale = head_dim ** (-0.5) * math.log2(math.e)
    mesh_id = pl.DeviceIdType.MESH
    has_left, has_right = me > 0, me < n - 1
    left, right = {"ctx": me - 1}, {"ctx": me + 1}

    def part(c):
        return pl.ds(pl.multiple_of(c * ROWS, ROWS), ROWS)

    def send_q(src, c, to, sems, own=False):
        return pltpu.make_async_remote_copy(
            src_ref=q_ref.at[part(c)] if own else qbuf.at[src, part(c)],
            dst_ref=qbuf.at[src, part(c)],
            send_sem=sems.at[src, c], recv_sem=q_recv.at[src, c],
            device_id=to, device_id_type=mesh_id,
        )

    def send_p(t, c, to, rx, rxs, sem, ssem):
        return (
            pltpu.make_async_remote_copy(
                src_ref=tx.at[t, part(c)], dst_ref=rx.at[t, part(c)],
                send_sem=p_send.at[t, c], recv_sem=sem.at[t, c],
                device_id=to, device_id_type=mesh_id,
            ),
            pltpu.make_async_remote_copy(
                src_ref=txs.at[t, c], dst_ref=rxs.at[t, c],
                send_sem=s_send.at[t, c], recv_sem=ssem.at[t, c],
                device_id=to, device_id_type=mesh_id,
            ),
        )

    to_right = (right, rxl, rxls, pl_recv, sl_recv)
    to_left = (left, rxr, rxrs, pr_recv, sr_recv)

    loads = [
        pltpu.make_async_copy(src, dst, local_sem.at[k])
        for k, (src, dst) in enumerate((
            (q_ref, qbuf.at[me]), (sk_ref, skbuf), (sv_ref, svbuf),
            (ck_ref, kbuf), (cv_ref, vbuf),
        ))
    ]
    for load in loads:
        load.start()

    barrier = pltpu.get_barrier_semaphore()

    @pl.when(has_left)
    def _():
        pl.semaphore_signal(barrier, inc=1, device_id=left, device_id_type=mesh_id)

    @pl.when(has_right)
    def _():
        pl.semaphore_signal(barrier, inc=1, device_id=right, device_id_type=mesh_id)

    pl.semaphore_wait(barrier, jnp.where(has_left, 1, 0) + jnp.where(has_right, 1, 0))

    for c in range(chunks):
        @pl.when(has_right)
        def _():
            send_q(me, c, right, q_right, True).start()

        @pl.when(has_left)
        def _():
            send_q(me, c, left, q_left, True).start()

    first_head = (lax.axis_index("head") * lax.axis_size("tp") + lax.axis_index("tp")) * kv_dev
    for j in range(qblocks):
        for g in range(kv_dev):
            found = [jnp.int32(0)] * per
            count = jnp.int32(0)
            for k in range(TOPK):
                slot = table_ref[picks_ref[j, first_head + g, k]]
                spot = slot - me * blocks_dev
                here = (spot >= 0) & (spot < blocks_dev)
                for r in range(per):
                    found[r] = jnp.where(here & (count == r), spot, found[r])
                count = count + jnp.where(here, 1, 0)
            for r in range(per):
                spots[j, g, r] = found[r]

    for load in loads:
        load.wait()

    def lanes(x):
        return [x[:, k:k + 128] for k in range(0, x.shape[1], 128)]

    def score(t, c, window):
        g = c // per_head
        j = t * tok // BLOCK
        picked = [spots[j, g, r] for r in range(per)]
        for h in range(ROWS // tok):
            at = pl.ds(pl.multiple_of(c * ROWS + h * tok, tok), tok)
            q = qbuf[t, at, :]
            parts = [
                lax.dot_general(
                    q, kbuf[g, spot], (((1,), (1,)), ((), ())),
                    preferred_element_type=jnp.float32,
                )
                for spot in picked
            ]
            if window:
                s = lax.dot_general(
                    q, skbuf[g], (((1,), (1,)), ((), ())),
                    preferred_element_type=jnp.float32,
                )
                row = lax.broadcasted_iota(jnp.int32, s.shape, 0)
                col = lax.broadcasted_iota(jnp.int32, s.shape, 1)
                own = jnp.where(t == me, 1, 0)
                lead = (row - col) * (2 * own - 1) + own
                parts.append(jnp.where(lead > 0, s, -jnp.inf))
            top = jnp.max(
                functools.reduce(jnp.maximum, [x for s in parts for x in lanes(s)]),
                axis=1, keepdims=True,
            ) * scale
            total = jnp.zeros((tok, head_dim), jnp.float32)
            sums = []
            for k, s in enumerate(parts):
                w = jnp.exp2(s * scale - top)
                sums.append(functools.reduce(jnp.add, lanes(w)))
                v = vbuf[g, picked[k]] if k < per else svbuf[g]
                total = total + jnp.dot(
                    w.astype(jnp.bfloat16), v, preferred_element_type=jnp.float32
                )
            acc[t, at, :] = total
            mcol[t, at, :] = top
            lcol[t, at, :] = jnp.sum(
                functools.reduce(jnp.add, sums), axis=1, keepdims=True
            )

    def compute(t, c):
        near = (t == me) | (t == me + 1)

        @pl.when(near)
        def _():
            score(t, c, True)

        @pl.when(jnp.logical_not(near))
        def _():
            score(t, c, False)

    eye = (
        lax.broadcasted_iota(jnp.int32, (128, 128), 0)
        == lax.broadcasted_iota(jnp.int32, (128, 128), 1)
    )

    def to_row(col):
        return jnp.sum(jnp.where(eye, col, 0.0), axis=0, keepdims=True)

    def to_col(row):
        return jnp.sum(jnp.where(eye, row, 0.0), axis=1, keepdims=True)

    cuts = ROWS // 128

    def at_cut(c, k):
        return pl.ds(pl.multiple_of(c * ROWS + k * 128, 128), 128)

    def own_part(t, c, k):
        at = at_cut(c, k)
        return acc[t, at, :], mcol[t, at, :], lcol[t, at, :]

    def merged(state, t, c, k, rx, rxs):
        return fold(
            *state, rx[t, at_cut(c, k), :].astype(jnp.int32).astype(jnp.float32),
            to_col(rxs[t, c, k:k + 1, :]), to_col(rxs[t, c, cuts + k:cuts + k + 1, :]),
        )

    def pack(state, t, c, k):
        a, m, l = state
        peak = jnp.maximum(jnp.max(jnp.abs(a), axis=1, keepdims=True), 1e-25)
        per_unit = 32767.0 / peak
        tx[t, at_cut(c, k), :] = jnp.round(a * per_unit).astype(jnp.int32).astype(jnp.int16)
        txs[t, c, k:k + 1, :] = to_row(m - jnp.log(per_unit) * math.log2(math.e))
        txs[t, c, cuts + k:cuts + k + 1, :] = to_row(l * per_unit)

    def hand_on(t, c, way, relay):
        if relay:
            for copy in send_p(t, c, *way):
                copy.wait_recv()
        for k in range(cuts):
            state = own_part(t, c, k)
            if relay:
                state = merged(state, t, c, k, way[1], way[2])
            pack(state, t, c, k)
        for copy in send_p(t, c, *way):
            copy.start()

    def each(body, count=chunks):
        lax.fori_loop(0, count, lambda c, z: (body(c), z)[1], 0)

    inner = has_left & has_right

    for b in range(1, n):
        def step(c, b=b):
            @pl.when(me >= b)
            def _():
                send_q(me - b, c, right, q_right).wait_recv()

                @pl.when(has_right)
                def _():
                    send_q(me - b, c, right, q_right).start()

            @pl.when(me + b < n)
            def _():
                send_q(me + b, c, left, q_left).wait_recv()

                @pl.when(has_left)
                def _():
                    send_q(me + b, c, left, q_left).start()

            @pl.when(me + b < n)
            def _():
                compute(me + b, c)

            @pl.when(me >= b)
            def _():
                compute(me - b, c)

            @pl.when(me == 0)
            def _():
                hand_on(b, c, to_right, False)

            @pl.when(me == n - 1)
            def _():
                hand_on(n - 1 - b, c, to_left, False)

            if b < n - 1:
                @pl.when(has_left & (me < b))
                def _():
                    hand_on(b, c, to_right, True)

                @pl.when(has_right & (me > n - 1 - b))
                def _():
                    hand_on(n - 1 - b, c, to_left, True)

        each(step)

    def last(k):
        c_right, c_left = k - (me - 1), k - (n - 2 - me)

        @pl.when(inner & (c_right >= 0) & (c_right < chunks))
        def _():
            hand_on(n - 1, c_right, to_right, True)

        @pl.when(inner & (c_left >= 0) & (c_left < chunks))
        def _():
            hand_on(0, c_left, to_left, True)

        @pl.when(k < chunks)
        def _():
            score(me, k, True)

    each(last, chunks + max(n - 3, 0))

    def finish(c):
        @pl.when(has_left)
        def _():
            for copy in send_p(me, c, *to_right):
                copy.wait_recv()

        @pl.when(has_right)
        def _():
            for copy in send_p(me, c, *to_left):
                copy.wait_recv()

        def close(from_left, from_right):
            for k in range(cuts):
                state = own_part(me, c, k)
                if from_left:
                    state = merged(state, me, c, k, rxl, rxls)
                if from_right:
                    state = merged(state, me, c, k, rxr, rxrs)
                out_ref[at_cut(c, k), :] = (state[0] / state[2]).astype(out_ref.dtype)

        for from_left in (False, True):
            for from_right in (False, True):
                @pl.when((has_left == from_left) & (has_right == from_right))
                def _():
                    close(from_left, from_right)

    each(finish)

    def drain(c):
        for s in range(n):
            @pl.when((s <= me) & has_right)
            def _():
                send_q(s, c, right, q_right).wait_send()

            @pl.when((s >= me) & has_left)
            def _():
                send_q(s, c, left, q_left).wait_send()

            @pl.when(s > me)
            def _():
                for copy in send_p(s, c, *to_right):
                    copy.wait_send()

            @pl.when(s < me)
            def _():
                for copy in send_p(s, c, *to_left):
                    copy.wait_send()

    each(drain)


def line_shards(
    queries, stretch_keys, stretch_values, cache_keys, cache_values, block_picks, block_table
):
    n = lax.axis_size("ctx")
    kv_dev, tok, head_dim = stretch_keys.shape
    rows = queries.shape[0] * tok
    chunks = rows // ROWS
    by_block = (kv_dev, cache_keys.shape[1] // BLOCK, BLOCK, head_dim)
    any_space = pl.BlockSpec(memory_space=pl.ANY)
    smem = pl.BlockSpec(memory_space=pltpu.SMEM)
    bf16, f32 = jnp.bfloat16, jnp.float32
    stats = pltpu.VMEM((n, chunks, 8, 128), f32)
    rows_bf16 = pltpu.VMEM((n, rows, head_dim), bf16)
    rows_int = pltpu.VMEM((n, rows, head_dim), jnp.int16)
    column = pltpu.VMEM((n, rows, 1), f32)
    sems = pltpu.SemaphoreType.DMA((n, chunks))
    result = pl.pallas_call(
        functools.partial(line_kernel, n, tok),
        out_shape=jax.ShapeDtypeStruct((rows, head_dim), bf16),
        in_specs=[smem, smem] + [any_space] * 5,
        out_specs=pl.BlockSpec(memory_space=pltpu.VMEM),
        scratch_shapes=[
            rows_bf16,
            pltpu.VMEM(by_block, bf16), pltpu.VMEM(by_block, bf16),
            pltpu.VMEM(stretch_keys.shape, bf16), pltpu.VMEM(stretch_values.shape, bf16),
            pltpu.VMEM((n, rows, head_dim), f32), column, column,
            rows_int, stats, rows_int, stats, rows_int, stats,
            pltpu.SMEM((block_picks.shape[0], kv_dev, TOPK // n), jnp.int32),
            pltpu.SemaphoreType.DMA((5,)),
        ] + [sems] * 9,
        compiler_params=pltpu.CompilerParams(
            collective_id=0, has_side_effects=True, vmem_limit_bytes=56 * 2**20
        ),
    )(
        block_picks, block_table, queries.reshape(rows, head_dim),
        stretch_keys, stretch_values, cache_keys.reshape(by_block), cache_values.reshape(by_block),
    )
    return result.reshape(queries.shape)


def solution(mesh):
    placed = (
        P(("head", "tp"), ("groups", "ctx"), None),
        P(("head", "tp"), ("groups", "ctx"), None),
        P(("head", "tp"), ("groups", "ctx"), None),
        P(("head", "tp"), ("groups", "ctx"), None),
        P(("head", "tp"), ("groups", "ctx"), None),
        P("groups", None, None),
        P("groups"),
    )
    few = TOPK % mesh.shape["ctx"] == 0
    return jax.shard_map(
        line_shards if few else shards,
        mesh=mesh,
        in_specs=placed,
        out_specs=P(("head", "tp"), ("groups", "ctx"), None),
        check_vma=False,
    )
```

```python
import functools
import math

import jax
import jax.numpy as jnp
import numpy as np
from jax import lax
from jax.experimental import pallas as pl
from jax.experimental.pallas import tpu as pltpu
from jax.sharding import PartitionSpec as P

BLOCK = 512
TOPK = 16


def shifted(value, axis, by):
    count = lax.axis_size(axis)
    pairs = [(i, i + by) for i in range(count) if 0 <= i + by < count]
    return lax.ppermute(value, axis, pairs)


def as_sent(value):

    def short(part):
        return part.astype(jnp.bfloat16) if part.dtype == jnp.float32 else part

    return jax.tree.map(short, value)


def partner(value, axis, bit):
    mask = 2**bit
    pairs = [(source, source ^ mask) for source in range(lax.axis_size(axis))]
    return lax.ppermute(value, axis, pairs)


def lookup(lookup_table, indices):
    entries = jnp.arange(lookup_table.shape[0], dtype=jnp.int32)
    return jnp.sum(jnp.where(indices[..., None] == entries, lookup_table, 0), axis=-1)


def owner_rank(owners):
    ordinal = jnp.arange(owners.shape[-1], dtype=jnp.int32)
    before = (owners[..., :, None] == owners[..., None, :]) & (ordinal[None, :] < ordinal[:, None])
    return jnp.sum(before, axis=-1)


def pick_rows(source, indices):
    return source[indices]


def take_blocks(blocks, indices):
    return jax.vmap(pick_rows)(blocks, indices)


def attend(query_rows, all_keys, all_values, allowed_mask):
    tile_relevance = jnp.einsum(
        "rd,kd->rk", query_rows, all_keys, preferred_element_type=jnp.float32
    )
    tile_relevance = tile_relevance * query_rows.shape[-1] ** (-0.5)
    tile_relevance = jnp.where(allowed_mask, tile_relevance, -jnp.inf)
    row_max = jnp.max(tile_relevance, axis=-1, keepdims=True)
    weights = jnp.exp(tile_relevance - row_max)
    weight_sum = jnp.sum(weights, axis=-1, keepdims=True)
    mixed = jnp.einsum(
        "rk,kd->rd", weights.astype(jnp.bfloat16), all_values, preferred_element_type=jnp.float32
    )
    return (mixed / weight_sum).astype(jnp.bfloat16)


def shards(
    queries, stretch_keys, stretch_values, cache_keys, cache_values, block_picks, block_table
):
    kv_dev, tok_dev, head_dim = stretch_keys.shape
    q_per_kv = queries.shape[0] // kv_dev
    blocks_dev = cache_keys.shape[1] // BLOCK
    ctx_size = lax.axis_size("ctx")
    ctx_index = lax.axis_index("ctx")
    per_peer = max(1, TOPK // ctx_size)
    parity = ctx_index % 2
    head_ids = lax.axis_index(("head", "tp")) * kv_dev + jnp.arange(kv_dev, dtype=jnp.int32)
    selector = head_ids[:, None] == jnp.arange(block_picks.shape[1], dtype=jnp.int32)[None, :]
    my_picks = jnp.sum(jnp.where(selector[None, :, :, None], block_picks[:, None, :, :], 0), axis=2)
    physical = lookup(block_table, my_picks)
    owners = physical // blocks_dev
    in_owner = physical % blocks_dev
    peer_rank = owner_rank(owners)
    targets = np.arange(ctx_size) * tok_dev // BLOCK
    target_owner = owners[targets]
    target_rank = peer_rank[targets]
    target_local = in_owner[targets]
    slot_ids = jnp.arange(per_peer, dtype=jnp.int32)
    matched = (target_owner[:, :, None, :] == ctx_index) & (
        target_rank[:, :, None, :] == slot_ids[None, None, :, None]
    )
    chosen = jnp.sum(jnp.where(matched, target_local[:, :, None, :], 0), axis=-1)
    usable = jnp.any(matched, axis=-1)
    chosen = jnp.transpose(chosen, (1, 0, 2)).reshape(kv_dev, ctx_size * per_peer)
    usable = jnp.transpose(usable, (1, 0, 2)).reshape(kv_dev, ctx_size * per_peer)
    my_block = ctx_index * tok_dev // BLOCK
    my_owner = lax.dynamic_index_in_dim(owners, my_block, 0, keepdims=False)
    my_rank = lax.dynamic_index_in_dim(peer_rank, my_block, 0, keepdims=False)
    my_slot = my_owner * per_peer + my_rank
    prev_keys, prev_values = shifted((stretch_keys, stretch_values), "ctx", 1)
    half_rows = BLOCK // 2
    key_halves = cache_keys.reshape(kv_dev, blocks_dev * 2, half_rows, head_dim)
    value_halves = cache_values.reshape(kv_dev, blocks_dev * 2, half_rows, head_dim)
    row_side = jnp.asarray(np.repeat(np.arange(ctx_size) % 2, per_peer), jnp.int32)
    half_index = chosen * 2 + row_side[None, :]
    sent_keys = jnp.where(usable[:, :, None, None], take_blocks(key_halves, half_index), 0).astype(
        jnp.bfloat16
    )
    sent_values = jnp.where(
        usable[:, :, None, None], take_blocks(value_halves, half_index), 0
    ).astype(jnp.bfloat16)
    got_keys, got_values = (
        lax.all_to_all(sent_keys, "ctx", split_axis=1, concat_axis=1, tiled=True),
        lax.all_to_all(sent_values, "ctx", split_axis=1, concat_axis=1, tiled=True),
    )
    mine_keys = take_blocks(got_keys, my_slot)
    mine_values = take_blocks(got_values, my_slot)
    other_keys, other_values = (
        partner(as_sent(mine_keys), "ctx", 0).astype(mine_keys.dtype),
        partner(as_sent(mine_values), "ctx", 0).astype(mine_values.dtype),
    )
    first_keys = jnp.where(parity == 0, mine_keys, other_keys)
    second_keys = jnp.where(parity == 0, other_keys, mine_keys)
    first_values = jnp.where(parity == 0, mine_values, other_values)
    second_values = jnp.where(parity == 0, other_values, mine_values)
    live_keys = jnp.concatenate([first_keys, second_keys], axis=2)
    live_values = jnp.concatenate([first_values, second_values], axis=2)
    span_cols = TOPK * BLOCK
    live_keys = live_keys.reshape(kv_dev, span_cols, head_dim)
    live_values = live_values.reshape(kv_dev, span_cols, head_dim)
    all_keys = jnp.concatenate([live_keys, prev_keys, stretch_keys], axis=1)
    all_values = jnp.concatenate([live_values, prev_values, stretch_values], axis=1)
    query_rows = queries.reshape(kv_dev, q_per_kv * tok_dev, head_dim)
    step_rows = min(512, q_per_kv * tok_dev)
    columns = jnp.arange(span_cols + 2 * tok_dev, dtype=jnp.int32)

    def one_head(packed):
        q_head, k_head, v_head = packed
        q_steps = q_head.reshape(-1, step_rows, head_dim)
        starts = jnp.arange(q_steps.shape[0], dtype=jnp.int32) * step_rows

        def one_step(packed_block_step):
            q_block, first_row = packed_block_step
            position = (first_row + jnp.arange(step_rows, dtype=jnp.int32)) % tok_dev
            cache_part = columns[None, :] < span_cols
            earlier_part = (
                (columns[None, :] >= span_cols)
                & (columns[None, :] < span_cols + tok_dev)
                & (columns[None, :] - span_cols > position[:, None])
                & (ctx_index > 0)
            )
            own_part = (columns[None, :] >= span_cols + tok_dev) & (
                columns[None, :] - span_cols - tok_dev <= position[:, None]
            )
            return attend(q_block, k_head, v_head, cache_part | earlier_part | own_part)

        return lax.map(one_step, (q_steps, starts)).reshape(q_per_kv * tok_dev, head_dim)

    result = lax.map(one_head, (query_rows, all_keys, all_values))
    return result.reshape(kv_dev * q_per_kv, tok_dev, head_dim)


ROWS = 512


def fold(a, m, l, a2, m2, l2):
    top = jnp.maximum(m, m2)
    x, y = jnp.exp2(m - top), jnp.exp2(m2 - top)
    return a * x + a2 * y, top, l * x + l2 * y


def line_kernel(
    n, tok, picks_ref, table_ref, q_ref, sk_ref, sv_ref, ck_ref, cv_ref, out_ref,
    qbuf, kbuf, vbuf, skbuf, svbuf, acc, mcol, lcol, tx, txs, rxl, rxls, rxr, rxrs,
    spots, local_sem, q_right, q_left, q_recv, p_send, s_send,
    pl_recv, sl_recv, pr_recv, sr_recv,
):
    me = lax.axis_index("ctx")
    rows, head_dim = q_ref.shape
    kv_dev, blocks_dev = ck_ref.shape[:2]
    chunks = rows // ROWS
    per_head = chunks // kv_dev
    per = TOPK // n
    qblocks = picks_ref.shape[0]
    scale = head_dim ** (-0.5) * math.log2(math.e)
    mesh_id = pl.DeviceIdType.MESH
    has_left, has_right = me > 0, me < n - 1
    left, right = {"ctx": me - 1}, {"ctx": me + 1}

    def part(c):
        return pl.ds(pl.multiple_of(c * ROWS, ROWS), ROWS)

    def send_q(src, c, to, sems, own=False):
        return pltpu.make_async_remote_copy(
            src_ref=q_ref.at[part(c)] if own else qbuf.at[src, part(c)],
            dst_ref=qbuf.at[src, part(c)],
            send_sem=sems.at[src, c], recv_sem=q_recv.at[src, c],
            device_id=to, device_id_type=mesh_id,
        )

    def send_p(t, c, to, rx, rxs, sem, ssem):
        return (
            pltpu.make_async_remote_copy(
                src_ref=tx.at[t, part(c)], dst_ref=rx.at[t, part(c)],
                send_sem=p_send.at[t, c], recv_sem=sem.at[t, c],
                device_id=to, device_id_type=mesh_id,
            ),
            pltpu.make_async_remote_copy(
                src_ref=txs.at[t, c], dst_ref=rxs.at[t, c],
                send_sem=s_send.at[t, c], recv_sem=ssem.at[t, c],
                device_id=to, device_id_type=mesh_id,
            ),
        )

    to_right = (right, rxl, rxls, pl_recv, sl_recv)
    to_left = (left, rxr, rxrs, pr_recv, sr_recv)

    loads = [
        pltpu.make_async_copy(src, dst, local_sem.at[k])
        for k, (src, dst) in enumerate((
            (q_ref, qbuf.at[me]), (sk_ref, skbuf), (sv_ref, svbuf),
            (ck_ref, kbuf), (cv_ref, vbuf),
        ))
    ]
    for load in loads:
        load.start()

    barrier = pltpu.get_barrier_semaphore()

    @pl.when(has_left)
    def _():
        pl.semaphore_signal(barrier, inc=1, device_id=left, device_id_type=mesh_id)

    @pl.when(has_right)
    def _():
        pl.semaphore_signal(barrier, inc=1, device_id=right, device_id_type=mesh_id)

    pl.semaphore_wait(barrier, jnp.where(has_left, 1, 0) + jnp.where(has_right, 1, 0))

    for c in range(chunks):
        @pl.when(has_right)
        def _():
            send_q(me, c, right, q_right, True).start()

        @pl.when(has_left)
        def _():
            send_q(me, c, left, q_left, True).start()

    first_head = (lax.axis_index("head") * lax.axis_size("tp") + lax.axis_index("tp")) * kv_dev
    for j in range(qblocks):
        for g in range(kv_dev):
            found = [jnp.int32(0)] * per
            count = jnp.int32(0)
            for k in range(TOPK):
                slot = table_ref[picks_ref[j, first_head + g, k]]
                spot = slot - me * blocks_dev
                here = (spot >= 0) & (spot < blocks_dev)
                for r in range(per):
                    found[r] = jnp.where(here & (count == r), spot, found[r])
                count = count + jnp.where(here, 1, 0)
            for r in range(per):
                spots[j, g, r] = found[r]

    for load in loads:
        load.wait()

    def lanes(x):
        return [x[:, k:k + 128] for k in range(0, x.shape[1], 128)]

    def score(t, c, window):
        g = c // per_head
        j = t * tok // BLOCK
        picked = [spots[j, g, r] for r in range(per)]
        heads = ROWS // tok
        at = [pl.ds(pl.multiple_of(c * ROWS + h * tok, tok), tok) for h in range(heads)]
        queries = [qbuf[t, rows_at, :] for rows_at in at]
        pieces = per + 1 if window else per

        def scores(h, k):
            s = lax.dot_general(
                queries[h], kbuf[g, picked[k]] if k < per else skbuf[g],
                (((1,), (1,)), ((), ())), preferred_element_type=jnp.float32,
            )
            if k < per:
                return s
            row = lax.broadcasted_iota(jnp.int32, s.shape, 0)
            col = lax.broadcasted_iota(jnp.int32, s.shape, 1)
            own = jnp.where(t == me, 1, 0)
            lead = (row - col) * (2 * own - 1) + own
            return jnp.where(lead > 0, s, -jnp.inf)

        parts = [scores(0, k) for k in range(pieces)]
        for h in range(heads):
            top = jnp.max(
                functools.reduce(jnp.maximum, [x for s in parts for x in lanes(s)]),
                axis=1, keepdims=True,
            ) * scale
            total = jnp.zeros((tok, head_dim), jnp.float32)
            sums, later = [], []
            for k, s in enumerate(parts):
                if h + 1 < heads:
                    later.append(scores(h + 1, k))
                w = jnp.exp2(s * scale - top)
                sums.append(functools.reduce(jnp.add, lanes(w)))
                v = vbuf[g, picked[k]] if k < per else svbuf[g]
                total = total + jnp.dot(
                    w.astype(jnp.bfloat16), v, preferred_element_type=jnp.float32
                )
            acc[t, at[h], :] = total
            mcol[t, at[h], :] = top
            lcol[t, at[h], :] = jnp.sum(
                functools.reduce(jnp.add, sums), axis=1, keepdims=True
            )
            parts = later

    def compute(t, c):
        near = (t == me) | (t == me + 1)

        @pl.when(near)
        def _():
            score(t, c, True)

        @pl.when(jnp.logical_not(near))
        def _():
            score(t, c, False)

    eye = (
        lax.broadcasted_iota(jnp.int32, (128, 128), 0)
        == lax.broadcasted_iota(jnp.int32, (128, 128), 1)
    )

    def to_row(col):
        return jnp.sum(jnp.where(eye, col, 0.0), axis=0, keepdims=True)

    def to_col(row):
        return jnp.sum(jnp.where(eye, row, 0.0), axis=1, keepdims=True)

    cuts = ROWS // 128

    def at_cut(c, k):
        return pl.ds(pl.multiple_of(c * ROWS + k * 128, 128), 128)

    def own_part(t, c, k):
        at = at_cut(c, k)
        return acc[t, at, :], mcol[t, at, :], lcol[t, at, :]

    def merged(state, t, c, k, rx, rxs):
        return fold(
            *state, rx[t, at_cut(c, k), :].astype(jnp.int32).astype(jnp.float32),
            to_col(rxs[t, c, k:k + 1, :]), to_col(rxs[t, c, cuts + k:cuts + k + 1, :]),
        )

    def pack(state, t, c, k):
        a, m, l = state
        peak = jnp.maximum(jnp.max(jnp.abs(a), axis=1, keepdims=True), 1e-25)
        per_unit = 32767.0 / peak
        tx[t, at_cut(c, k), :] = jnp.round(a * per_unit).astype(jnp.int32).astype(jnp.int16)
        txs[t, c, k:k + 1, :] = to_row(m - jnp.log(per_unit) * math.log2(math.e))
        txs[t, c, cuts + k:cuts + k + 1, :] = to_row(l * per_unit)

    def hand_on(t, c, way, relay):
        if relay:
            for copy in send_p(t, c, *way):
                copy.wait_recv()
        for k in range(cuts):
            state = own_part(t, c, k)
            if relay:
                state = merged(state, t, c, k, way[1], way[2])
            pack(state, t, c, k)
        for copy in send_p(t, c, *way):
            copy.start()

    def each(body, count=chunks):
        lax.fori_loop(0, count, lambda c, z: (body(c), z)[1], 0)

    inner = has_left & has_right

    for b in range(1, n):
        def step(c, b=b):
            @pl.when(me >= b)
            def _():
                send_q(me - b, c, right, q_right).wait_recv()

                @pl.when(has_right)
                def _():
                    send_q(me - b, c, right, q_right).start()

            @pl.when(me + b < n)
            def _():
                send_q(me + b, c, left, q_left).wait_recv()

                @pl.when(has_left)
                def _():
                    send_q(me + b, c, left, q_left).start()

            @pl.when(me + b < n)
            def _():
                compute(me + b, c)

            @pl.when(me >= b)
            def _():
                compute(me - b, c)

            @pl.when(me == 0)
            def _():
                hand_on(b, c, to_right, False)

            @pl.when(me == n - 1)
            def _():
                hand_on(n - 1 - b, c, to_left, False)

            if b < n - 1:
                @pl.when(has_left & (me < b))
                def _():
                    hand_on(b, c, to_right, True)

                @pl.when(has_right & (me > n - 1 - b))
                def _():
                    hand_on(n - 1 - b, c, to_left, True)

        each(step)

    def last(k):
        c_right, c_left = k - (me - 1), k - (n - 2 - me)

        @pl.when(inner & (c_right >= 0) & (c_right < chunks))
        def _():
            hand_on(n - 1, c_right, to_right, True)

        @pl.when(inner & (c_left >= 0) & (c_left < chunks))
        def _():
            hand_on(0, c_left, to_left, True)

        @pl.when(k < chunks)
        def _():
            score(me, k, True)

    each(last, chunks + max(n - 3, 0))

    def finish(c):
        @pl.when(has_left)
        def _():
            for copy in send_p(me, c, *to_right):
                copy.wait_recv()

        @pl.when(has_right)
        def _():
            for copy in send_p(me, c, *to_left):
                copy.wait_recv()

        def close(from_left, from_right):
            for k in range(cuts):
                state = own_part(me, c, k)
                if from_left:
                    state = merged(state, me, c, k, rxl, rxls)
                if from_right:
                    state = merged(state, me, c, k, rxr, rxrs)
                out_ref[at_cut(c, k), :] = (state[0] / state[2]).astype(out_ref.dtype)

        for from_left in (False, True):
            for from_right in (False, True):
                @pl.when((has_left == from_left) & (has_right == from_right))
                def _():
                    close(from_left, from_right)

    each(finish)

    def drain(c):
        for s in range(n):
            @pl.when((s <= me) & has_right)
            def _():
                send_q(s, c, right, q_right).wait_send()

            @pl.when((s >= me) & has_left)
            def _():
                send_q(s, c, left, q_left).wait_send()

            @pl.when(s > me)
            def _():
                for copy in send_p(s, c, *to_right):
                    copy.wait_send()

            @pl.when(s < me)
            def _():
                for copy in send_p(s, c, *to_left):
                    copy.wait_send()

    each(drain)


def line_shards(
    queries, stretch_keys, stretch_values, cache_keys, cache_values, block_picks, block_table
):
    n = lax.axis_size("ctx")
    kv_dev, tok, head_dim = stretch_keys.shape
    rows = queries.shape[0] * tok
    chunks = rows // ROWS
    by_block = (kv_dev, cache_keys.shape[1] // BLOCK, BLOCK, head_dim)
    any_space = pl.BlockSpec(memory_space=pl.ANY)
    smem = pl.BlockSpec(memory_space=pltpu.SMEM)
    bf16, f32 = jnp.bfloat16, jnp.float32
    stats = pltpu.VMEM((n, chunks, 8, 128), f32)
    rows_bf16 = pltpu.VMEM((n, rows, head_dim), bf16)
    rows_int = pltpu.VMEM((n, rows, head_dim), jnp.int16)
    column = pltpu.VMEM((n, rows, 1), f32)
    sems = pltpu.SemaphoreType.DMA((n, chunks))
    result = pl.pallas_call(
        functools.partial(line_kernel, n, tok),
        out_shape=jax.ShapeDtypeStruct((rows, head_dim), bf16),
        in_specs=[smem, smem] + [any_space] * 5,
        out_specs=pl.BlockSpec(memory_space=pltpu.VMEM),
        scratch_shapes=[
            rows_bf16,
            pltpu.VMEM(by_block, bf16), pltpu.VMEM(by_block, bf16),
            pltpu.VMEM(stretch_keys.shape, bf16), pltpu.VMEM(stretch_values.shape, bf16),
            pltpu.VMEM((n, rows, head_dim), f32), column, column,
            rows_int, stats, rows_int, stats, rows_int, stats,
            pltpu.SMEM((block_picks.shape[0], kv_dev, TOPK // n), jnp.int32),
            pltpu.SemaphoreType.DMA((5,)),
        ] + [sems] * 9,
        compiler_params=pltpu.CompilerParams(
            collective_id=0, has_side_effects=True, vmem_limit_bytes=56 * 2**20
        ),
    )(
        block_picks, block_table, queries.reshape(rows, head_dim),
        stretch_keys, stretch_values, cache_keys.reshape(by_block), cache_values.reshape(by_block),
    )
    return result.reshape(queries.shape)


def solution(mesh):
    placed = (
        P(("head", "tp"), ("groups", "ctx"), None),
        P(("head", "tp"), ("groups", "ctx"), None),
        P(("head", "tp"), ("groups", "ctx"), None),
        P(("head", "tp"), ("groups", "ctx"), None),
        P(("head", "tp"), ("groups", "ctx"), None),
        P("groups", None, None),
        P("groups"),
    )
    few = TOPK % mesh.shape["ctx"] == 0
    return jax.shard_map(
        line_shards if few else shards,
        mesh=mesh,
        in_specs=placed,
        out_specs=P(("head", "tp"), ("groups", "ctx"), None),
        check_vma=False,
    )
```

```python
import functools
import math

import jax
import jax.numpy as jnp
import numpy as np
from jax import lax
from jax.experimental import pallas as pl
from jax.experimental.pallas import tpu as pltpu
from jax.sharding import PartitionSpec as P

BLOCK = 512
TOPK = 16


def shifted(value, axis, by):
    count = lax.axis_size(axis)
    pairs = [(i, i + by) for i in range(count) if 0 <= i + by < count]
    return lax.ppermute(value, axis, pairs)


def as_sent(value):

    def short(part):
        return part.astype(jnp.bfloat16) if part.dtype == jnp.float32 else part

    return jax.tree.map(short, value)


def partner(value, axis, bit):
    mask = 2**bit
    pairs = [(source, source ^ mask) for source in range(lax.axis_size(axis))]
    return lax.ppermute(value, axis, pairs)


def lookup(lookup_table, indices):
    entries = jnp.arange(lookup_table.shape[0], dtype=jnp.int32)
    return jnp.sum(jnp.where(indices[..., None] == entries, lookup_table, 0), axis=-1)


def owner_rank(owners):
    ordinal = jnp.arange(owners.shape[-1], dtype=jnp.int32)
    before = (owners[..., :, None] == owners[..., None, :]) & (ordinal[None, :] < ordinal[:, None])
    return jnp.sum(before, axis=-1)


def pick_rows(source, indices):
    return source[indices]


def take_blocks(blocks, indices):
    return jax.vmap(pick_rows)(blocks, indices)


def attend(query_rows, all_keys, all_values, allowed_mask):
    tile_relevance = jnp.einsum(
        "rd,kd->rk", query_rows, all_keys, preferred_element_type=jnp.float32
    )
    tile_relevance = tile_relevance * query_rows.shape[-1] ** (-0.5)
    tile_relevance = jnp.where(allowed_mask, tile_relevance, -jnp.inf)
    row_max = jnp.max(tile_relevance, axis=-1, keepdims=True)
    weights = jnp.exp(tile_relevance - row_max)
    weight_sum = jnp.sum(weights, axis=-1, keepdims=True)
    mixed = jnp.einsum(
        "rk,kd->rd", weights.astype(jnp.bfloat16), all_values, preferred_element_type=jnp.float32
    )
    return (mixed / weight_sum).astype(jnp.bfloat16)


def shards(
    queries, stretch_keys, stretch_values, cache_keys, cache_values, block_picks, block_table
):
    kv_dev, tok_dev, head_dim = stretch_keys.shape
    q_per_kv = queries.shape[0] // kv_dev
    blocks_dev = cache_keys.shape[1] // BLOCK
    ctx_size = lax.axis_size("ctx")
    ctx_index = lax.axis_index("ctx")
    per_peer = max(1, TOPK // ctx_size)
    parity = ctx_index % 2
    head_ids = lax.axis_index(("head", "tp")) * kv_dev + jnp.arange(kv_dev, dtype=jnp.int32)
    selector = head_ids[:, None] == jnp.arange(block_picks.shape[1], dtype=jnp.int32)[None, :]
    my_picks = jnp.sum(jnp.where(selector[None, :, :, None], block_picks[:, None, :, :], 0), axis=2)
    physical = lookup(block_table, my_picks)
    owners = physical // blocks_dev
    in_owner = physical % blocks_dev
    peer_rank = owner_rank(owners)
    targets = np.arange(ctx_size) * tok_dev // BLOCK
    target_owner = owners[targets]
    target_rank = peer_rank[targets]
    target_local = in_owner[targets]
    slot_ids = jnp.arange(per_peer, dtype=jnp.int32)
    matched = (target_owner[:, :, None, :] == ctx_index) & (
        target_rank[:, :, None, :] == slot_ids[None, None, :, None]
    )
    chosen = jnp.sum(jnp.where(matched, target_local[:, :, None, :], 0), axis=-1)
    usable = jnp.any(matched, axis=-1)
    chosen = jnp.transpose(chosen, (1, 0, 2)).reshape(kv_dev, ctx_size * per_peer)
    usable = jnp.transpose(usable, (1, 0, 2)).reshape(kv_dev, ctx_size * per_peer)
    my_block = ctx_index * tok_dev // BLOCK
    my_owner = lax.dynamic_index_in_dim(owners, my_block, 0, keepdims=False)
    my_rank = lax.dynamic_index_in_dim(peer_rank, my_block, 0, keepdims=False)
    my_slot = my_owner * per_peer + my_rank
    prev_keys, prev_values = shifted((stretch_keys, stretch_values), "ctx", 1)
    half_rows = BLOCK // 2
    key_halves = cache_keys.reshape(kv_dev, blocks_dev * 2, half_rows, head_dim)
    value_halves = cache_values.reshape(kv_dev, blocks_dev * 2, half_rows, head_dim)
    row_side = jnp.asarray(np.repeat(np.arange(ctx_size) % 2, per_peer), jnp.int32)
    half_index = chosen * 2 + row_side[None, :]
    sent_keys = jnp.where(usable[:, :, None, None], take_blocks(key_halves, half_index), 0).astype(
        jnp.bfloat16
    )
    sent_values = jnp.where(
        usable[:, :, None, None], take_blocks(value_halves, half_index), 0
    ).astype(jnp.bfloat16)
    got_keys, got_values = (
        lax.all_to_all(sent_keys, "ctx", split_axis=1, concat_axis=1, tiled=True),
        lax.all_to_all(sent_values, "ctx", split_axis=1, concat_axis=1, tiled=True),
    )
    mine_keys = take_blocks(got_keys, my_slot)
    mine_values = take_blocks(got_values, my_slot)
    other_keys, other_values = (
        partner(as_sent(mine_keys), "ctx", 0).astype(mine_keys.dtype),
        partner(as_sent(mine_values), "ctx", 0).astype(mine_values.dtype),
    )
    first_keys = jnp.where(parity == 0, mine_keys, other_keys)
    second_keys = jnp.where(parity == 0, other_keys, mine_keys)
    first_values = jnp.where(parity == 0, mine_values, other_values)
    second_values = jnp.where(parity == 0, other_values, mine_values)
    live_keys = jnp.concatenate([first_keys, second_keys], axis=2)
    live_values = jnp.concatenate([first_values, second_values], axis=2)
    span_cols = TOPK * BLOCK
    live_keys = live_keys.reshape(kv_dev, span_cols, head_dim)
    live_values = live_values.reshape(kv_dev, span_cols, head_dim)
    all_keys = jnp.concatenate([live_keys, prev_keys, stretch_keys], axis=1)
    all_values = jnp.concatenate([live_values, prev_values, stretch_values], axis=1)
    query_rows = queries.reshape(kv_dev, q_per_kv * tok_dev, head_dim)
    step_rows = min(512, q_per_kv * tok_dev)
    columns = jnp.arange(span_cols + 2 * tok_dev, dtype=jnp.int32)

    def one_head(packed):
        q_head, k_head, v_head = packed
        q_steps = q_head.reshape(-1, step_rows, head_dim)
        starts = jnp.arange(q_steps.shape[0], dtype=jnp.int32) * step_rows

        def one_step(packed_block_step):
            q_block, first_row = packed_block_step
            position = (first_row + jnp.arange(step_rows, dtype=jnp.int32)) % tok_dev
            cache_part = columns[None, :] < span_cols
            earlier_part = (
                (columns[None, :] >= span_cols)
                & (columns[None, :] < span_cols + tok_dev)
                & (columns[None, :] - span_cols > position[:, None])
                & (ctx_index > 0)
            )
            own_part = (columns[None, :] >= span_cols + tok_dev) & (
                columns[None, :] - span_cols - tok_dev <= position[:, None]
            )
            return attend(q_block, k_head, v_head, cache_part | earlier_part | own_part)

        return lax.map(one_step, (q_steps, starts)).reshape(q_per_kv * tok_dev, head_dim)

    result = lax.map(one_head, (query_rows, all_keys, all_values))
    return result.reshape(kv_dev * q_per_kv, tok_dev, head_dim)


ROWS = 512


def fold(a, m, l, a2, m2, l2):
    top = jnp.maximum(m, m2)
    x, y = jnp.exp2(m - top), jnp.exp2(m2 - top)
    return a * x + a2 * y, top, l * x + l2 * y


def line_kernel(
    n, tok, picks_ref, table_ref, q_ref, sk_ref, sv_ref, ck_ref, cv_ref, out_ref,
    qbuf, kbuf, vbuf, skbuf, svbuf, acc, mcol, lcol, tx, txs, rxl, rxls, rxr, rxrs,
    spots, local_sem, q_right, q_left, q_recv, p_send, s_send,
    pl_recv, sl_recv, pr_recv, sr_recv,
):
    me = lax.axis_index("ctx")
    rows, head_dim = q_ref.shape
    kv_dev, blocks_dev = ck_ref.shape[:2]
    chunks = rows // ROWS
    head_rows = rows // kv_dev
    heads = ROWS // tok
    early = heads // 2
    per = TOPK // n
    qblocks = picks_ref.shape[0]
    scale = head_dim ** (-0.5) * math.log2(math.e)
    mesh_id = pl.DeviceIdType.MESH
    has_left, has_right = me > 0, me < n - 1
    left, right = {"ctx": me - 1}, {"ctx": me + 1}

    def part(c):
        return pl.ds(pl.multiple_of(c * ROWS, ROWS), ROWS)

    def send_q(src, c, to, sems, own=False):
        return pltpu.make_async_remote_copy(
            src_ref=q_ref.at[part(c)] if own else qbuf.at[src, part(c)],
            dst_ref=qbuf.at[src, part(c)],
            send_sem=sems.at[src, c], recv_sem=q_recv.at[src, c],
            device_id=to, device_id_type=mesh_id,
        )

    def send_p(t, c, to, rx, rxs, sem, ssem):
        return (
            pltpu.make_async_remote_copy(
                src_ref=tx.at[t, part(c)], dst_ref=rx.at[t, part(c)],
                send_sem=p_send.at[t, c], recv_sem=sem.at[t, c],
                device_id=to, device_id_type=mesh_id,
            ),
            pltpu.make_async_remote_copy(
                src_ref=txs.at[t, c], dst_ref=rxs.at[t, c],
                send_sem=s_send.at[t, c], recv_sem=ssem.at[t, c],
                device_id=to, device_id_type=mesh_id,
            ),
        )

    to_right = (right, rxl, rxls, pl_recv, sl_recv)
    to_left = (left, rxr, rxrs, pr_recv, sr_recv)

    loads = [
        pltpu.make_async_copy(src, dst, local_sem.at[k])
        for k, (src, dst) in enumerate((
            (q_ref, qbuf.at[me]), (sk_ref, skbuf), (sv_ref, svbuf),
            (ck_ref, kbuf), (cv_ref, vbuf),
        ))
    ]
    for load in loads:
        load.start()

    barrier = pltpu.get_barrier_semaphore()

    @pl.when(has_left)
    def _():
        pl.semaphore_signal(barrier, inc=1, device_id=left, device_id_type=mesh_id)

    @pl.when(has_right)
    def _():
        pl.semaphore_signal(barrier, inc=1, device_id=right, device_id_type=mesh_id)

    pl.semaphore_wait(barrier, jnp.where(has_left, 1, 0) + jnp.where(has_right, 1, 0))

    for c in range(chunks):
        @pl.when(has_right)
        def _():
            send_q(me, c, right, q_right, True).start()

        @pl.when(has_left)
        def _():
            send_q(me, c, left, q_left, True).start()

    first_head = (lax.axis_index("head") * lax.axis_size("tp") + lax.axis_index("tp")) * kv_dev
    for j in range(qblocks):
        for g in range(kv_dev):
            found = [jnp.int32(0)] * per
            count = jnp.int32(0)
            for k in range(TOPK):
                slot = table_ref[picks_ref[j, first_head + g, k]]
                spot = slot - me * blocks_dev
                here = (spot >= 0) & (spot < blocks_dev)
                for r in range(per):
                    found[r] = jnp.where(here & (count == r), spot, found[r])
                count = count + jnp.where(here, 1, 0)
            for r in range(per):
                spots[j, g, r] = found[r]

    for load in loads:
        load.wait()

    def lanes(x):
        return [x[:, k:k + 128] for k in range(0, x.shape[1], 128)]

    def score(t, start, heads, window):
        g = start // head_rows
        j = t * tok // BLOCK
        picked = [spots[j, g, r] for r in range(per)]
        at = [pl.ds(pl.multiple_of(start + h * tok, tok), tok) for h in range(heads)]
        queries = [qbuf[t, rows_at, :] for rows_at in at]
        pieces = per + 1 if window else per

        def scores(h, k):
            s = lax.dot_general(
                queries[h], kbuf[g, picked[k]] if k < per else skbuf[g],
                (((1,), (1,)), ((), ())), preferred_element_type=jnp.float32,
            )
            if k < per:
                return s
            row = lax.broadcasted_iota(jnp.int32, s.shape, 0)
            col = lax.broadcasted_iota(jnp.int32, s.shape, 1)
            own = jnp.where(t == me, 1, 0)
            lead = (row - col) * (2 * own - 1) + own
            return jnp.where(lead > 0, s, -jnp.inf)

        parts = [scores(0, k) for k in range(pieces)]
        for h in range(heads):
            top = jnp.max(
                functools.reduce(jnp.maximum, [x for s in parts for x in lanes(s)]),
                axis=1, keepdims=True,
            ) * scale
            total = jnp.zeros((tok, head_dim), jnp.float32)
            sums, later = [], []
            for k, s in enumerate(parts):
                if h + 1 < heads:
                    later.append(scores(h + 1, k))
                w = jnp.exp2(s * scale - top)
                sums.append(functools.reduce(jnp.add, lanes(w)))
                v = vbuf[g, picked[k]] if k < per else svbuf[g]
                total = total + jnp.dot(
                    w.astype(jnp.bfloat16), v, preferred_element_type=jnp.float32
                )
            acc[t, at[h], :] = total
            mcol[t, at[h], :] = top
            lcol[t, at[h], :] = jnp.sum(
                functools.reduce(jnp.add, sums), axis=1, keepdims=True
            )
            parts = later

    def compute(t, c):
        near = (t == me) | (t == me + 1)

        @pl.when(near)
        def _():
            score(t, c * ROWS, heads, True)

        @pl.when(jnp.logical_not(near))
        def _():
            score(t, c * ROWS, heads, False)

    eye = (
        lax.broadcasted_iota(jnp.int32, (128, 128), 0)
        == lax.broadcasted_iota(jnp.int32, (128, 128), 1)
    )

    def to_row(col):
        return jnp.sum(jnp.where(eye, col, 0.0), axis=0, keepdims=True)

    def to_col(row):
        return jnp.sum(jnp.where(eye, row, 0.0), axis=1, keepdims=True)

    cuts = ROWS // 128

    def at_cut(c, k):
        return pl.ds(pl.multiple_of(c * ROWS + k * 128, 128), 128)

    def own_part(t, c, k):
        at = at_cut(c, k)
        return acc[t, at, :], mcol[t, at, :], lcol[t, at, :]

    def merged(state, t, c, k, rx, rxs):
        return fold(
            *state, rx[t, at_cut(c, k), :].astype(jnp.int32).astype(jnp.float32),
            to_col(rxs[t, c, k:k + 1, :]), to_col(rxs[t, c, cuts + k:cuts + k + 1, :]),
        )

    def pack(state, t, c, k):
        a, m, l = state
        peak = jnp.maximum(jnp.max(jnp.abs(a), axis=1, keepdims=True), 1e-25)
        per_unit = 32767.0 / peak
        tx[t, at_cut(c, k), :] = jnp.round(a * per_unit).astype(jnp.int32).astype(jnp.int16)
        txs[t, c, k:k + 1, :] = to_row(m - jnp.log(per_unit) * math.log2(math.e))
        txs[t, c, cuts + k:cuts + k + 1, :] = to_row(l * per_unit)

    def hand_on(t, c, way, relay):
        if relay:
            for copy in send_p(t, c, *way):
                copy.wait_recv()
        for k in range(cuts):
            state = own_part(t, c, k)
            if relay:
                state = merged(state, t, c, k, way[1], way[2])
            pack(state, t, c, k)
        for copy in send_p(t, c, *way):
            copy.start()

    def each(body, count=chunks):
        lax.fori_loop(0, count, lambda c, z: (body(c), z)[1], 0)

    inner = has_left & has_right

    def own_head(u):
        score(me, u * tok, 1, True)

    each(own_head, early * chunks)

    for b in range(1, n):
        def receive(c, b=b):
            @pl.when(me >= b)
            def _():
                send_q(me - b, c, right, q_right).wait_recv()

                @pl.when(has_right)
                def _():
                    send_q(me - b, c, right, q_right).start()

            @pl.when(me + b < n)
            def _():
                send_q(me + b, c, left, q_left).wait_recv()

                @pl.when(has_left)
                def _():
                    send_q(me + b, c, left, q_left).start()

        def step(c, b=b, receive=receive):
            if b == 1:
                receive(c)
            else:
                pl.when(jnp.logical_not(inner))(lambda: receive(c))

            @pl.when(me + b < n)
            def _():
                compute(me + b, c)

            @pl.when(me >= b)
            def _():
                compute(me - b, c)

            @pl.when(me == 0)
            def _():
                hand_on(b, c, to_right, False)

            @pl.when(me == n - 1)
            def _():
                hand_on(n - 1 - b, c, to_left, False)

            if b < n - 1:
                @pl.when(has_left & (me < b))
                def _():
                    hand_on(b, c, to_right, True)

                @pl.when(has_right & (me > n - 1 - b))
                def _():
                    hand_on(n - 1 - b, c, to_left, True)

        if b > 1:
            pl.when(inner)(lambda: each(receive))
        each(step)

    def last(k):
        c_right, c_left = k - (me - 1), k - (n - 2 - me)

        @pl.when(inner & (c_right >= 0) & (c_right < chunks))
        def _():
            hand_on(n - 1, c_right, to_right, True)

        @pl.when(inner & (c_left >= 0) & (c_left < chunks))
        def _():
            hand_on(0, c_left, to_left, True)

        @pl.when(k < chunks)
        def _():
            for h in range(early, heads):
                own_head(early * chunks + k * (heads - early) + h - early)

    each(last, chunks + max(n - 3, 0))

    def finish(c):
        @pl.when(has_left)
        def _():
            for copy in send_p(me, c, *to_right):
                copy.wait_recv()

        @pl.when(has_right)
        def _():
            for copy in send_p(me, c, *to_left):
                copy.wait_recv()

        def close(from_left, from_right):
            for k in range(cuts):
                state = own_part(me, c, k)
                if from_left:
                    state = merged(state, me, c, k, rxl, rxls)
                if from_right:
                    state = merged(state, me, c, k, rxr, rxrs)
                out_ref[at_cut(c, k), :] = (state[0] / state[2]).astype(out_ref.dtype)

        for from_left in (False, True):
            for from_right in (False, True):
                @pl.when((has_left == from_left) & (has_right == from_right))
                def _():
                    close(from_left, from_right)

    each(finish)

    def drain(c):
        for s in range(n):
            @pl.when((s <= me) & has_right)
            def _():
                send_q(s, c, right, q_right).wait_send()

            @pl.when((s >= me) & has_left)
            def _():
                send_q(s, c, left, q_left).wait_send()

            @pl.when(s > me)
            def _():
                for copy in send_p(s, c, *to_right):
                    copy.wait_send()

            @pl.when(s < me)
            def _():
                for copy in send_p(s, c, *to_left):
                    copy.wait_send()

    each(drain)


def line_shards(
    queries, stretch_keys, stretch_values, cache_keys, cache_values, block_picks, block_table
):
    n = lax.axis_size("ctx")
    kv_dev, tok, head_dim = stretch_keys.shape
    rows = queries.shape[0] * tok
    chunks = rows // ROWS
    by_block = (kv_dev, cache_keys.shape[1] // BLOCK, BLOCK, head_dim)
    any_space = pl.BlockSpec(memory_space=pl.ANY)
    smem = pl.BlockSpec(memory_space=pltpu.SMEM)
    bf16, f32 = jnp.bfloat16, jnp.float32
    stats = pltpu.VMEM((n, chunks, 8, 128), f32)
    rows_bf16 = pltpu.VMEM((n, rows, head_dim), bf16)
    rows_int = pltpu.VMEM((n, rows, head_dim), jnp.int16)
    column = pltpu.VMEM((n, rows, 1), f32)
    sems = pltpu.SemaphoreType.DMA((n, chunks))
    result = pl.pallas_call(
        functools.partial(line_kernel, n, tok),
        out_shape=jax.ShapeDtypeStruct((rows, head_dim), bf16),
        in_specs=[smem, smem] + [any_space] * 5,
        out_specs=pl.BlockSpec(memory_space=pltpu.VMEM),
        scratch_shapes=[
            rows_bf16,
            pltpu.VMEM(by_block, bf16), pltpu.VMEM(by_block, bf16),
            pltpu.VMEM(stretch_keys.shape, bf16), pltpu.VMEM(stretch_values.shape, bf16),
            pltpu.VMEM((n, rows, head_dim), f32), column, column,
            rows_int, stats, rows_int, stats, rows_int, stats,
            pltpu.SMEM((block_picks.shape[0], kv_dev, TOPK // n), jnp.int32),
            pltpu.SemaphoreType.DMA((5,)),
        ] + [sems] * 9,
        compiler_params=pltpu.CompilerParams(
            collective_id=0, has_side_effects=True, vmem_limit_bytes=56 * 2**20
        ),
    )(
        block_picks, block_table, queries.reshape(rows, head_dim),
        stretch_keys, stretch_values, cache_keys.reshape(by_block), cache_values.reshape(by_block),
    )
    return result.reshape(queries.shape)


def solution(mesh):
    placed = (
        P(("head", "tp"), ("groups", "ctx"), None),
        P(("head", "tp"), ("groups", "ctx"), None),
        P(("head", "tp"), ("groups", "ctx"), None),
        P(("head", "tp"), ("groups", "ctx"), None),
        P(("head", "tp"), ("groups", "ctx"), None),
        P("groups", None, None),
        P("groups"),
    )
    few = TOPK % mesh.shape["ctx"] == 0
    return jax.shard_map(
        line_shards if few else shards,
        mesh=mesh,
        in_specs=placed,
        out_specs=P(("head", "tp"), ("groups", "ctx"), None),
        check_vma=False,
    )
```

```python
import functools
import math

import jax
import jax.numpy as jnp
import numpy as np
from jax import lax
from jax.experimental import pallas as pl
from jax.experimental.pallas import tpu as pltpu
from jax.sharding import PartitionSpec as P

BLOCK = 512
TOPK = 16


def shifted(value, axis, by):
    count = lax.axis_size(axis)
    pairs = [(i, i + by) for i in range(count) if 0 <= i + by < count]
    return lax.ppermute(value, axis, pairs)


def as_sent(value):

    def short(part):
        return part.astype(jnp.bfloat16) if part.dtype == jnp.float32 else part

    return jax.tree.map(short, value)


def partner(value, axis, bit):
    mask = 2**bit
    pairs = [(source, source ^ mask) for source in range(lax.axis_size(axis))]
    return lax.ppermute(value, axis, pairs)


def lookup(lookup_table, indices):
    entries = jnp.arange(lookup_table.shape[0], dtype=jnp.int32)
    return jnp.sum(jnp.where(indices[..., None] == entries, lookup_table, 0), axis=-1)


def owner_rank(owners):
    ordinal = jnp.arange(owners.shape[-1], dtype=jnp.int32)
    before = (owners[..., :, None] == owners[..., None, :]) & (ordinal[None, :] < ordinal[:, None])
    return jnp.sum(before, axis=-1)


def pick_rows(source, indices):
    return source[indices]


def take_blocks(blocks, indices):
    return jax.vmap(pick_rows)(blocks, indices)


def attend(query_rows, all_keys, all_values, allowed_mask):
    tile_relevance = jnp.einsum(
        "rd,kd->rk", query_rows, all_keys, preferred_element_type=jnp.float32
    )
    tile_relevance = tile_relevance * query_rows.shape[-1] ** (-0.5)
    tile_relevance = jnp.where(allowed_mask, tile_relevance, -jnp.inf)
    row_max = jnp.max(tile_relevance, axis=-1, keepdims=True)
    weights = jnp.exp(tile_relevance - row_max)
    weight_sum = jnp.sum(weights, axis=-1, keepdims=True)
    mixed = jnp.einsum(
        "rk,kd->rd", weights.astype(jnp.bfloat16), all_values, preferred_element_type=jnp.float32
    )
    return (mixed / weight_sum).astype(jnp.bfloat16)


def shards(
    queries, stretch_keys, stretch_values, cache_keys, cache_values, block_picks, block_table
):
    kv_dev, tok_dev, head_dim = stretch_keys.shape
    q_per_kv = queries.shape[0] // kv_dev
    blocks_dev = cache_keys.shape[1] // BLOCK
    ctx_size = lax.axis_size("ctx")
    ctx_index = lax.axis_index("ctx")
    per_peer = max(1, TOPK // ctx_size)
    parity = ctx_index % 2
    head_ids = lax.axis_index(("head", "tp")) * kv_dev + jnp.arange(kv_dev, dtype=jnp.int32)
    selector = head_ids[:, None] == jnp.arange(block_picks.shape[1], dtype=jnp.int32)[None, :]
    my_picks = jnp.sum(jnp.where(selector[None, :, :, None], block_picks[:, None, :, :], 0), axis=2)
    physical = lookup(block_table, my_picks)
    owners = physical // blocks_dev
    in_owner = physical % blocks_dev
    peer_rank = owner_rank(owners)
    targets = np.arange(ctx_size) * tok_dev // BLOCK
    target_owner = owners[targets]
    target_rank = peer_rank[targets]
    target_local = in_owner[targets]
    slot_ids = jnp.arange(per_peer, dtype=jnp.int32)
    matched = (target_owner[:, :, None, :] == ctx_index) & (
        target_rank[:, :, None, :] == slot_ids[None, None, :, None]
    )
    chosen = jnp.sum(jnp.where(matched, target_local[:, :, None, :], 0), axis=-1)
    usable = jnp.any(matched, axis=-1)
    chosen = jnp.transpose(chosen, (1, 0, 2)).reshape(kv_dev, ctx_size * per_peer)
    usable = jnp.transpose(usable, (1, 0, 2)).reshape(kv_dev, ctx_size * per_peer)
    my_block = ctx_index * tok_dev // BLOCK
    my_owner = lax.dynamic_index_in_dim(owners, my_block, 0, keepdims=False)
    my_rank = lax.dynamic_index_in_dim(peer_rank, my_block, 0, keepdims=False)
    my_slot = my_owner * per_peer + my_rank
    prev_keys, prev_values = shifted((stretch_keys, stretch_values), "ctx", 1)
    half_rows = BLOCK // 2
    key_halves = cache_keys.reshape(kv_dev, blocks_dev * 2, half_rows, head_dim)
    value_halves = cache_values.reshape(kv_dev, blocks_dev * 2, half_rows, head_dim)
    row_side = jnp.asarray(np.repeat(np.arange(ctx_size) % 2, per_peer), jnp.int32)
    half_index = chosen * 2 + row_side[None, :]
    sent_keys = jnp.where(usable[:, :, None, None], take_blocks(key_halves, half_index), 0).astype(
        jnp.bfloat16
    )
    sent_values = jnp.where(
        usable[:, :, None, None], take_blocks(value_halves, half_index), 0
    ).astype(jnp.bfloat16)
    got_keys, got_values = (
        lax.all_to_all(sent_keys, "ctx", split_axis=1, concat_axis=1, tiled=True),
        lax.all_to_all(sent_values, "ctx", split_axis=1, concat_axis=1, tiled=True),
    )
    mine_keys = take_blocks(got_keys, my_slot)
    mine_values = take_blocks(got_values, my_slot)
    other_keys, other_values = (
        partner(as_sent(mine_keys), "ctx", 0).astype(mine_keys.dtype),
        partner(as_sent(mine_values), "ctx", 0).astype(mine_values.dtype),
    )
    first_keys = jnp.where(parity == 0, mine_keys, other_keys)
    second_keys = jnp.where(parity == 0, other_keys, mine_keys)
    first_values = jnp.where(parity == 0, mine_values, other_values)
    second_values = jnp.where(parity == 0, other_values, mine_values)
    live_keys = jnp.concatenate([first_keys, second_keys], axis=2)
    live_values = jnp.concatenate([first_values, second_values], axis=2)
    span_cols = TOPK * BLOCK
    live_keys = live_keys.reshape(kv_dev, span_cols, head_dim)
    live_values = live_values.reshape(kv_dev, span_cols, head_dim)
    all_keys = jnp.concatenate([live_keys, prev_keys, stretch_keys], axis=1)
    all_values = jnp.concatenate([live_values, prev_values, stretch_values], axis=1)
    query_rows = queries.reshape(kv_dev, q_per_kv * tok_dev, head_dim)
    step_rows = min(512, q_per_kv * tok_dev)
    columns = jnp.arange(span_cols + 2 * tok_dev, dtype=jnp.int32)

    def one_head(packed):
        q_head, k_head, v_head = packed
        q_steps = q_head.reshape(-1, step_rows, head_dim)
        starts = jnp.arange(q_steps.shape[0], dtype=jnp.int32) * step_rows

        def one_step(packed_block_step):
            q_block, first_row = packed_block_step
            position = (first_row + jnp.arange(step_rows, dtype=jnp.int32)) % tok_dev
            cache_part = columns[None, :] < span_cols
            earlier_part = (
                (columns[None, :] >= span_cols)
                & (columns[None, :] < span_cols + tok_dev)
                & (columns[None, :] - span_cols > position[:, None])
                & (ctx_index > 0)
            )
            own_part = (columns[None, :] >= span_cols + tok_dev) & (
                columns[None, :] - span_cols - tok_dev <= position[:, None]
            )
            return attend(q_block, k_head, v_head, cache_part | earlier_part | own_part)

        return lax.map(one_step, (q_steps, starts)).reshape(q_per_kv * tok_dev, head_dim)

    result = lax.map(one_head, (query_rows, all_keys, all_values))
    return result.reshape(kv_dev * q_per_kv, tok_dev, head_dim)


ROWS = 256


def fold(a, m, l, a2, m2, l2):
    top = jnp.maximum(m, m2)
    x, y = jnp.exp2(m - top), jnp.exp2(m2 - top)
    return a * x + a2 * y, top, l * x + l2 * y


def line_kernel(
    n, tok, picks_ref, table_ref, q_ref, sk_ref, sv_ref, ck_ref, cv_ref, out_ref,
    qbuf, kbuf, vbuf, skbuf, svbuf, acc, mcol, lcol, tx, txs, rxl, rxls, rxr, rxrs,
    spots, local_sem, q_right, q_left, q_recv, p_send, s_send,
    pl_recv, sl_recv, pr_recv, sr_recv,
):
    me = lax.axis_index("ctx")
    rows, head_dim = q_ref.shape
    kv_dev, blocks_dev = ck_ref.shape[:2]
    chunks = rows // ROWS
    head_rows = rows // kv_dev
    heads = ROWS // tok
    own_heads = rows // tok
    early = own_heads // 2
    per = TOPK // n
    qblocks = picks_ref.shape[0]
    scale = head_dim ** (-0.5) * math.log2(math.e)
    mesh_id = pl.DeviceIdType.MESH
    has_left, has_right = me > 0, me < n - 1
    left, right = {"ctx": me - 1}, {"ctx": me + 1}

    def part(c):
        return pl.ds(pl.multiple_of(c * ROWS, ROWS), ROWS)

    def send_q(src, c, to, sems, own=False):
        return pltpu.make_async_remote_copy(
            src_ref=q_ref.at[part(c)] if own else qbuf.at[src, part(c)],
            dst_ref=qbuf.at[src, part(c)],
            send_sem=sems.at[src, c], recv_sem=q_recv.at[src, c],
            device_id=to, device_id_type=mesh_id,
        )

    def send_p(t, c, to, rx, rxs, sem, ssem):
        return (
            pltpu.make_async_remote_copy(
                src_ref=tx.at[t, part(c)], dst_ref=rx.at[t, part(c)],
                send_sem=p_send.at[t, c], recv_sem=sem.at[t, c],
                device_id=to, device_id_type=mesh_id,
            ),
            pltpu.make_async_remote_copy(
                src_ref=txs.at[t, c], dst_ref=rxs.at[t, c],
                send_sem=s_send.at[t, c], recv_sem=ssem.at[t, c],
                device_id=to, device_id_type=mesh_id,
            ),
        )

    to_right = (right, rxl, rxls, pl_recv, sl_recv)
    to_left = (left, rxr, rxrs, pr_recv, sr_recv)

    loads = [
        pltpu.make_async_copy(src, dst, local_sem.at[k])
        for k, (src, dst) in enumerate((
            (q_ref, qbuf.at[me]), (sk_ref, skbuf), (sv_ref, svbuf),
            (ck_ref, kbuf), (cv_ref, vbuf),
        ))
    ]
    for load in loads:
        load.start()

    barrier = pltpu.get_barrier_semaphore()

    @pl.when(has_left)
    def _():
        pl.semaphore_signal(barrier, inc=1, device_id=left, device_id_type=mesh_id)

    @pl.when(has_right)
    def _():
        pl.semaphore_signal(barrier, inc=1, device_id=right, device_id_type=mesh_id)

    pl.semaphore_wait(barrier, jnp.where(has_left, 1, 0) + jnp.where(has_right, 1, 0))

    for c in range(chunks):
        @pl.when(has_right)
        def _():
            send_q(me, c, right, q_right, True).start()

        @pl.when(has_left)
        def _():
            send_q(me, c, left, q_left, True).start()

    first_head = (lax.axis_index("head") * lax.axis_size("tp") + lax.axis_index("tp")) * kv_dev
    for j in range(qblocks):
        for g in range(kv_dev):
            found = [jnp.int32(0)] * per
            count = jnp.int32(0)
            for k in range(TOPK):
                slot = table_ref[picks_ref[j, first_head + g, k]]
                spot = slot - me * blocks_dev
                here = (spot >= 0) & (spot < blocks_dev)
                for r in range(per):
                    found[r] = jnp.where(here & (count == r), spot, found[r])
                count = count + jnp.where(here, 1, 0)
            for r in range(per):
                spots[j, g, r] = found[r]

    for load in loads:
        load.wait()

    def lanes(x):
        return [x[:, k:k + 128] for k in range(0, x.shape[1], 128)]

    def score(t, start, heads, window):
        g = start // head_rows
        j = t * tok // BLOCK
        picked = [spots[j, g, r] for r in range(per)]
        at = [pl.ds(pl.multiple_of(start + h * tok, tok), tok) for h in range(heads)]
        queries = [qbuf[t, rows_at, :] for rows_at in at]
        pieces = per + 1 if window else per

        def scores(h, k):
            s = lax.dot_general(
                queries[h], kbuf[g, picked[k]] if k < per else skbuf[g],
                (((1,), (1,)), ((), ())), preferred_element_type=jnp.float32,
            )
            if k < per:
                return s
            row = lax.broadcasted_iota(jnp.int32, s.shape, 0)
            col = lax.broadcasted_iota(jnp.int32, s.shape, 1)
            own = jnp.where(t == me, 1, 0)
            lead = (row - col) * (2 * own - 1) + own
            return jnp.where(lead > 0, s, -jnp.inf)

        parts = [scores(0, k) for k in range(pieces)]
        for h in range(heads):
            top = jnp.max(
                functools.reduce(jnp.maximum, [x for s in parts for x in lanes(s)]),
                axis=1, keepdims=True,
            ) * scale
            total = jnp.zeros((tok, head_dim), jnp.float32)
            sums, later = [], []
            for k, s in enumerate(parts):
                if h + 1 < heads:
                    later.append(scores(h + 1, k))
                w = jnp.exp2(s * scale - top)
                sums.append(functools.reduce(jnp.add, lanes(w)))
                v = vbuf[g, picked[k]] if k < per else svbuf[g]
                total = total + jnp.dot(
                    w.astype(jnp.bfloat16), v, preferred_element_type=jnp.float32
                )
            acc[t, at[h], :] = total
            mcol[t, at[h], :] = top
            lcol[t, at[h], :] = jnp.sum(
                functools.reduce(jnp.add, sums), axis=1, keepdims=True
            )
            parts = later

    def compute(t, c):
        near = (t == me) | (t == me + 1)

        @pl.when(near)
        def _():
            score(t, c * ROWS, heads, True)

        @pl.when(jnp.logical_not(near))
        def _():
            score(t, c * ROWS, heads, False)

    eye = (
        lax.broadcasted_iota(jnp.int32, (128, 128), 0)
        == lax.broadcasted_iota(jnp.int32, (128, 128), 1)
    )

    def to_row(col):
        return jnp.sum(jnp.where(eye, col, 0.0), axis=0, keepdims=True)

    def to_col(row):
        return jnp.sum(jnp.where(eye, row, 0.0), axis=1, keepdims=True)

    cuts = ROWS // 128

    def at_cut(c, k):
        return pl.ds(pl.multiple_of(c * ROWS + k * 128, 128), 128)

    def own_part(t, c, k):
        at = at_cut(c, k)
        return acc[t, at, :], mcol[t, at, :], lcol[t, at, :]

    def merged(state, t, c, k, rx, rxs):
        return fold(
            *state, rx[t, at_cut(c, k), :].astype(jnp.int32).astype(jnp.float32),
            to_col(rxs[t, c, k:k + 1, :]), to_col(rxs[t, c, cuts + k:cuts + k + 1, :]),
        )

    def pack(state, t, c, k):
        a, m, l = state
        peak = jnp.maximum(jnp.max(jnp.abs(a), axis=1, keepdims=True), 1e-25)
        per_unit = 32767.0 / peak
        tx[t, at_cut(c, k), :] = jnp.round(a * per_unit).astype(jnp.int32).astype(jnp.int16)
        txs[t, c, k:k + 1, :] = to_row(m - jnp.log(per_unit) * math.log2(math.e))
        txs[t, c, cuts + k:cuts + k + 1, :] = to_row(l * per_unit)

    def hand_on(t, c, way, relay):
        if relay:
            for copy in send_p(t, c, *way):
                copy.wait_recv()
        for k in range(cuts):
            state = own_part(t, c, k)
            if relay:
                state = merged(state, t, c, k, way[1], way[2])
            pack(state, t, c, k)
        for copy in send_p(t, c, *way):
            copy.start()

    def each(body, count=chunks):
        lax.fori_loop(0, count, lambda c, z: (body(c), z)[1], 0)

    inner = has_left & has_right

    def own_head(u):
        score(me, u * tok, 1, True)

    each(own_head, early)

    for b in range(1, n):
        def receive(c, b=b):
            @pl.when(me >= b)
            def _():
                send_q(me - b, c, right, q_right).wait_recv()

                @pl.when(has_right)
                def _():
                    send_q(me - b, c, right, q_right).start()

            @pl.when(me + b < n)
            def _():
                send_q(me + b, c, left, q_left).wait_recv()

                @pl.when(has_left)
                def _():
                    send_q(me + b, c, left, q_left).start()

        def step(c, b=b, receive=receive):
            if b == 1:
                receive(c)
            else:
                pl.when(jnp.logical_not(inner))(lambda: receive(c))

            @pl.when(me + b < n)
            def _():
                compute(me + b, c)

            @pl.when(me >= b)
            def _():
                compute(me - b, c)

            @pl.when(me == 0)
            def _():
                hand_on(b, c, to_right, False)

            @pl.when(me == n - 1)
            def _():
                hand_on(n - 1 - b, c, to_left, False)

            if b < n - 1:
                @pl.when(has_left & (me < b))
                def _():
                    hand_on(b, c, to_right, True)

                @pl.when(has_right & (me > n - 1 - b))
                def _():
                    hand_on(n - 1 - b, c, to_left, True)

        if b > 1:
            pl.when(inner)(lambda: each(receive))
        each(step)

    def last(k):
        c_right, c_left = k - (me - 1), k - (n - 2 - me)

        @pl.when(inner & (c_right >= 0) & (c_right < chunks))
        def _():
            hand_on(n - 1, c_right, to_right, True)

        @pl.when(inner & (c_left >= 0) & (c_left < chunks))
        def _():
            hand_on(0, c_left, to_left, True)

        @pl.when(k < own_heads - early)
        def _():
            own_head(early + k)

    each(last, max(chunks + max(n - 3, 0), own_heads - early))

    def finish(c):
        @pl.when(has_left)
        def _():
            for copy in send_p(me, c, *to_right):
                copy.wait_recv()

        @pl.when(has_right)
        def _():
            for copy in send_p(me, c, *to_left):
                copy.wait_recv()

        def close(from_left, from_right):
            for k in range(cuts):
                state = own_part(me, c, k)
                if from_left:
                    state = merged(state, me, c, k, rxl, rxls)
                if from_right:
                    state = merged(state, me, c, k, rxr, rxrs)
                out_ref[at_cut(c, k), :] = (state[0] / state[2]).astype(out_ref.dtype)

        for from_left in (False, True):
            for from_right in (False, True):
                @pl.when((has_left == from_left) & (has_right == from_right))
                def _():
                    close(from_left, from_right)

    each(finish)

    def drain(c):
        for s in range(n):
            @pl.when((s <= me) & has_right)
            def _():
                send_q(s, c, right, q_right).wait_send()

            @pl.when((s >= me) & has_left)
            def _():
                send_q(s, c, left, q_left).wait_send()

            @pl.when(s > me)
            def _():
                for copy in send_p(s, c, *to_right):
                    copy.wait_send()

            @pl.when(s < me)
            def _():
                for copy in send_p(s, c, *to_left):
                    copy.wait_send()

    each(drain)


def line_shards(
    queries, stretch_keys, stretch_values, cache_keys, cache_values, block_picks, block_table
):
    n = lax.axis_size("ctx")
    kv_dev, tok, head_dim = stretch_keys.shape
    rows = queries.shape[0] * tok
    chunks = rows // ROWS
    by_block = (kv_dev, cache_keys.shape[1] // BLOCK, BLOCK, head_dim)
    any_space = pl.BlockSpec(memory_space=pl.ANY)
    smem = pl.BlockSpec(memory_space=pltpu.SMEM)
    bf16, f32 = jnp.bfloat16, jnp.float32
    stats = pltpu.VMEM((n, chunks, 2 * ROWS // 128, 128), f32)
    rows_bf16 = pltpu.VMEM((n, rows, head_dim), bf16)
    rows_int = pltpu.VMEM((n, rows, head_dim), jnp.int16)
    column = pltpu.VMEM((n, rows, 1), f32)
    sems = pltpu.SemaphoreType.DMA((n, chunks))
    result = pl.pallas_call(
        functools.partial(line_kernel, n, tok),
        out_shape=jax.ShapeDtypeStruct((rows, head_dim), bf16),
        in_specs=[smem, smem] + [any_space] * 5,
        out_specs=pl.BlockSpec(memory_space=pltpu.VMEM),
        scratch_shapes=[
            rows_bf16,
            pltpu.VMEM(by_block, bf16), pltpu.VMEM(by_block, bf16),
            pltpu.VMEM(stretch_keys.shape, bf16), pltpu.VMEM(stretch_values.shape, bf16),
            pltpu.VMEM((n, rows, head_dim), f32), column, column,
            rows_int, stats, rows_int, stats, rows_int, stats,
            pltpu.SMEM((block_picks.shape[0], kv_dev, TOPK // n), jnp.int32),
            pltpu.SemaphoreType.DMA((5,)),
        ] + [sems] * 9,
        compiler_params=pltpu.CompilerParams(
            collective_id=0, has_side_effects=True, vmem_limit_bytes=56 * 2**20
        ),
    )(
        block_picks, block_table, queries.reshape(rows, head_dim),
        stretch_keys, stretch_values, cache_keys.reshape(by_block), cache_values.reshape(by_block),
    )
    return result.reshape(queries.shape)


def solution(mesh):
    placed = (
        P(("head", "tp"), ("groups", "ctx"), None),
        P(("head", "tp"), ("groups", "ctx"), None),
        P(("head", "tp"), ("groups", "ctx"), None),
        P(("head", "tp"), ("groups", "ctx"), None),
        P(("head", "tp"), ("groups", "ctx"), None),
        P("groups", None, None),
        P("groups"),
    )
    few = TOPK % mesh.shape["ctx"] == 0
    return jax.shard_map(
        line_shards if few else shards,
        mesh=mesh,
        in_specs=placed,
        out_specs=P(("head", "tp"), ("groups", "ctx"), None),
        check_vma=False,
    )
```
